1024 devices in a mesh: group: 16 (over z), expert: 64 (over x, y, core).
Axes of the slice: x: 4, y: 8, z: 16, core: 2. Of those that a mesh axis runs over, the one named last changes fastest.
Arguments:
- grad_out: bfloat16 [64, 48, 4096], P('expert', 'group'), may hold values from -2 to 2
- inputs: bfloat16 [64, 48, 4096], P('expert', 'group'), may hold values from -6 to 6
- expert_ids: int32 [64, 48, 8], P('expert'), may hold values from 0 to 127, all different within a row; in each aligned block of 48 rows (0 to 47, 48 to 95, ..., all dimensions but the last counted through in order) at most 4 rows name the same one
- route_weights: float32 [64, 48, 8], P('expert'), may hold values from 0.05 to 1
- w_gate: bfloat16 [1024, 512, 1024], P(('group', 'expert')), may hold values from -0.09375 to 0.09375
- w_up: bfloat16 [1024, 512, 1024], P(('group', 'expert')), may hold values from -0.09375 to 0.09375
- w_down: bfloat16 [1024, 1024, 512], P(('group', 'expert')), may hold values from -0.1875 to 0.1875
Outputs:
- grad_in: float32 [64, 48, 4096], P('expert', 'group')
- grad_route: float32 [64, 48, 8], P('expert', 'group')
The draws below stay inside these ranges and needn't reach their ends.
Inputs may be any that keep to these rules, and one draw needn't show every extreme that they name: `expert_ids`: each token names 8 different experts; expert e belongs to group e // 8. Among the 48 tokens of one index of the expert axis (one aligned block of the leading dimensions) no expert is named more than 4 times, a bound that some block reaches.
All inputs are finite; a program needn't handle non-finite values.
Results may differ from the reference program's by a relative error of at most 0.0029.
Values may be sent and summed in bfloat16 or wider, within the bound.
No kernel may reach another device: no remote copies, remote signals or barrier semaphores. Data moves between devices by JAX's collectives and lax.ppermute only.
A program may use at most 32 MiB of HBM per device.

```python
import math
import jax
import jax.numpy as jnp
import numpy as np
from jax import lax

D = 4096
HID = 1024
TOP = 8
SLICES = 8
DS = 512
EXPERTS = 128
TOK_COL = 48
TOKENS = 3072
MOST = 4
N_EXPERT = 64


def level_of(rng, extent, pieces, low, high):
    loudness = 1.0
    for position, parts in pieces:
        heights = jax.random.uniform(jax.random.fold_in(jax.random.fold_in(rng, 6), position), (parts,), jnp.float32, low / len(pieces), high / len(pieces))
        loudness = loudness * jnp.repeat(jnp.exp(heights), extent[position] // parts).reshape((-1,) + (1,) * (len(extent) - 1 - position))
    return loudness


def deal_out(own_key, own, number, rows, number_of, top, reach, lean):
    order = jax.random.permutation(own_key, number_of)
    crowded, usual = portions_of(number_of, rows * top, reach, lean, True), portions_of(number_of, rows * top, reach, lean, False)
    places = jnp.arange(number_of)

    def named(sizes, rotation):
        used = int((sizes > 0).sum())
        fixed = max(1, used // 4)
        shifted = fixed + (places - fixed + rotation * (used - fixed)) % max(1, number_of - fixed)
        return jnp.zeros((number_of,), jnp.int32).at[order[jnp.where(places < fixed, places, shifted)]].set(jnp.asarray(sizes, jnp.int32))

    sizes = jnp.where(number % 4 == 0, named(crowded, number // 4), named(usual, number - number // 4 - 1))
    mixed = jax.random.permutation(jax.random.fold_in(own, 3), number_of)
    donor, sink = mixed[0:number_of // 2 * 2:2], mixed[1:number_of // 2 * 2:2]
    room = jnp.minimum(sizes[donor] - 1, reach - sizes[sink]) // 2
    room = jnp.where((donor == order[0]) | (sink == order[0]) | (sizes[sink] == 0), 0, jnp.maximum(room, 0))
    shifted = jax.random.randint(jax.random.fold_in(own, 4), (number_of // 2,), 0, 1 << 20) % (room + 1)
    sizes = sizes.at[donor].add(-shifted).at[sink].add(shifted)
    items = jnp.searchsorted(jnp.cumsum(sizes), jnp.arange(rows * top), side="right").astype(jnp.int32)
    table = items.reshape(top, rows).T
    table = table[jax.random.permutation(jax.random.fold_in(own, 1), rows)]
    rotation = jax.random.randint(jax.random.fold_in(own, 2), (rows, 1), 0, top)
    return jnp.take_along_axis(table, (jnp.arange(top)[None, :] + rotation) % top, axis=1)


def portions_of(number_of, total, bound, lean, full):
    portions = [(1 << 20) // math.isqrt(rank ** lean) + 1 for rank in range(1, number_of + 1)]
    largest = bound if full else min(bound, max(-(-total // number_of), total * portions[0] // sum(portions)))
    least = 1 if total - largest >= number_of - 1 else 0
    holding, spare = [largest] + [least] * (number_of - 1), total - largest - least * (number_of - 1)
    while spare > 0:
        free = [i for i in range(1, number_of) if holding[i] < largest] or [i for i in range(1, number_of) if holding[i] < bound]
        pool, remaining = sum([portions[i] for i in free]), spare
        for i in free:
            addition = min(bound - holding[i], max(1, remaining * portions[i] // pool), spare)
            holding[i] = holding[i] + addition
            spare = spare - addition
    return np.array(holding)


def scatter_about(own_key, shape, spread, most, pieces=(), kind=jnp.bfloat16):
    result = jax.random.normal(own_key, shape, jnp.float32) * spread
    if len(pieces) > 0:
        result = level_of(own_key, shape, pieces, -0.22, 0.18) * result
    return jnp.clip(result, min=-most, max=most).astype(kind)


def setup_inputs(seed: int = 0) -> dict:
    arg_keys = jax.random.split(jax.random.key(seed), 8)
    grad_out = scatter_about(arg_keys[0], (N_EXPERT, TOK_COL, D), 0.3, 2.0, ((0, 64), (1, 16)))
    inputs = scatter_about(arg_keys[1], (N_EXPERT, TOK_COL, D), 1.0, 6.0, ((0, 64), (1, 16)))
    expert_ids_keys = jax.random.split(jax.random.fold_in(arg_keys[2], 1), N_EXPERT * TOK_COL // TOK_COL)
    expert_ids_turns = jax.random.permutation(jax.random.fold_in(arg_keys[2], 3), N_EXPERT * TOK_COL // TOK_COL)
    expert_ids = jax.vmap(lambda own, number: deal_out(jax.random.fold_in(arg_keys[2], 2), own, number, TOK_COL, EXPERTS, TOP, MOST, 2))(expert_ids_keys, expert_ids_turns).reshape((N_EXPERT, TOK_COL, TOP))
    route_weights = jnp.clip(jnp.exp(math.log(1.0) - 2.9957323 * jax.random.uniform(arg_keys[3], (N_EXPERT, TOK_COL, TOP), jnp.float32) ** level_of(arg_keys[3], (N_EXPERT, TOK_COL, TOP), ((0, 64),), -0.2, 0.2)), 0.05, 1.0)
    w_gate = scatter_about(arg_keys[4], (EXPERTS * SLICES, DS, HID), D ** -0.5, 0.09375, ((0, 1024),))
    w_up = scatter_about(arg_keys[5], (EXPERTS * SLICES, DS, HID), D ** -0.5, 0.09375, ((0, 1024),))
    w_down = scatter_about(arg_keys[6], (EXPERTS * SLICES, HID, DS), HID ** -0.5, 0.1875, ((0, 1024),))
    return {"grad_out": grad_out, "inputs": inputs, "expert_ids": expert_ids, "route_weights": route_weights, "w_gate": w_gate, "w_up": w_up, "w_down": w_down}


def silu_slope(value):
    sig = jax.nn.sigmoid(value)
    return sig * (1.0 + value * (1.0 - sig))


def reference(grad_out, inputs, expert_ids, route_weights, w_gate, w_up, w_down):
    grad_rows = grad_out.reshape(TOKENS, D)
    input_rows = inputs.reshape(TOKENS, D)
    flat_ids = expert_ids.reshape(TOKENS * TOP)
    flat_weights = route_weights.reshape(TOKENS * TOP)
    capacity = N_EXPERT * MOST

    def one_expert(carry, expert):
        grad_total, route_total = carry
        matches = flat_ids == expert
        positions = jnp.nonzero(matches, size=capacity, fill_value=0)[0].astype(jnp.int32)
        count = jnp.sum(matches.astype(jnp.int32))
        valid = (jnp.arange(capacity, dtype=jnp.int32) < count).astype(jnp.float32)
        token_idx = positions // TOP
        first = (expert * SLICES).astype(jnp.int32)
        gate_full = lax.dynamic_slice_in_dim(w_gate, first, SLICES, 0).reshape(D, HID)
        up_full = lax.dynamic_slice_in_dim(w_up, first, SLICES, 0).reshape(D, HID)
        down_full = lax.dynamic_slice_in_dim(w_down, first, SLICES, 0)
        down_full = jnp.transpose(down_full, (1, 0, 2)).reshape(HID, D)
        picked_x = input_rows[token_idx]
        picked_grad = grad_rows[token_idx]
        gate_sum = jnp.dot(picked_x, gate_full, preferred_element_type=jnp.float32)
        up_sum = jnp.dot(picked_x, up_full, preferred_element_type=jnp.float32)
        down_sum = jnp.dot(picked_grad, down_full.T, preferred_element_type=jnp.float32)
        hidden_val = jax.nn.silu(gate_sum) * up_sum
        route_grad = jnp.sum(hidden_val * down_sum, axis=1)
        grad_gate = (down_sum * up_sum * silu_slope(gate_sum)).astype(jnp.bfloat16)
        grad_up = (down_sum * jax.nn.silu(gate_sum)).astype(jnp.bfloat16)
        grad_x = jnp.dot(grad_gate, gate_full.T, preferred_element_type=jnp.float32)
        grad_x = grad_x + jnp.dot(grad_up, up_full.T, preferred_element_type=jnp.float32)
        scaled = flat_weights[positions] * valid
        grad_total = grad_total.at[token_idx].add(grad_x * scaled[:, None])
        route_total = route_total.at[positions].add(route_grad * valid)
        return (grad_total, route_total), None

    start = (jnp.zeros((TOKENS, D), jnp.float32), jnp.zeros((TOKENS * TOP,), jnp.float32))
    (grad_total, route_total), _ = lax.scan(one_expert, start, jnp.arange(EXPERTS, dtype=jnp.int32))
    return grad_total.reshape(N_EXPERT, TOK_COL, D), route_total.reshape(N_EXPERT, TOK_COL, TOP)
```

```python
import functools

import jax
import jax.numpy as jnp
from jax import lax
from jax.experimental import pallas as pl
from jax.experimental.pallas import tpu as pltpu
from jax.sharding import Mesh, PartitionSpec as P

BF = jnp.bfloat16
F32 = jnp.float32
MOST = 4
SPLIT = 8
ROWS = 2 * MOST
CORES = ("x", "yh", "yl", "c")
CHIPS = ("x", "yh", "yl")
ABT = (((1,), (1,)), ((), ()))


def dot(a, b):
    return jnp.dot(a, b, preferred_element_type=F32)


def dot_t(a, b):
    return lax.dot_general(a, b, ABT, preferred_element_type=F32)


def iota(shape, axis):
    return lax.broadcasted_iota(jnp.int32, shape, axis)


def call(kernel, out, limit_mib, *args, smem=0):
    spaces = [pltpu.SMEM] * smem + [pltpu.VMEM] * (len(args) - smem)
    many = isinstance(out, (list, tuple))
    outs = [pl.BlockSpec(memory_space=pltpu.VMEM) for _ in out] if many else None
    return pl.pallas_call(
        kernel,
        out_shape=out,
        in_specs=[pl.BlockSpec(memory_space=space) for space in spaces],
        out_specs=outs if many else pl.BlockSpec(memory_space=pltpu.VMEM),
        compiler_params=pltpu.CompilerParams(vmem_limit_bytes=limit_mib << 20),
    )(*args)


def payload_kernel(toks, width, x_ref, g_ref, o_ref):
    for tensor, ref in enumerate((x_ref, g_ref)):
        value = ref[...].astype(F32)
        for t in range(toks):
            rows = [value[t : t + 1, s * width : (s + 1) * width] for s in range(SPLIT)]
            at = (t * 2 + tensor) * width
            o_ref[:, at : at + width] = jnp.concatenate(rows, axis=0).astype(BF)


def rank_table(ids, first, experts):
    column = ids.shape[0]
    lane = iota((column, experts), 1)
    match = jnp.zeros((column, experts), F32)
    for e in range(experts):
        named = jnp.sum((ids == first + e).astype(F32), axis=1, keepdims=True)
        match = match + jnp.where(lane == e, named, 0.0)
    earlier = (iota((column, column), 1) < iota((column, column), 0)).astype(BF)
    rank = dot(earlier, match.astype(BF))
    return jnp.where(match > 0.0, rank, -1.0)


def row_fields(index, chips_y):
    slot = index % MOST
    part = (index // MOST) % (2 * chips_y)
    return index // (MOST * 2 * chips_y), part, slot


def pick_kernel(toks, experts, chips_y, first_ref, ids_ref, o_ref):
    _, rows, lanes = o_ref.shape
    column = ids_ref.shape[0]
    rank = rank_table(ids_ref[...], first_ref[0], experts).astype(BF)
    expert, _, _ = row_fields(iota((rows, experts), 0), chips_y)
    spread = dot_t((expert == iota((rows, experts), 1)).astype(BF), rank).astype(BF)
    _, part, slot = row_fields(iota((rows, lanes), 0), chips_y)
    same_part = part == iota((rows, lanes), 1) % SPLIT
    tok = iota((column, lanes), 0)
    group = iota((column, lanes), 1) // SPLIT
    for t in range(toks):
        table = dot(spread, (tok == group * toks + t).astype(BF))
        o_ref[t] = (same_part & (table == slot.astype(F32))).astype(BF)


def merge_kernel(toks, experts, chips_y, first_ref, ids_ref, w_ref, hi_ref, lo_ref, pick_ref):
    _, rows, lanes = hi_ref.shape
    column = ids_ref.shape[0]
    ids = ids_ref[...]
    first = first_ref[0]
    rank = rank_table(ids, first, experts).astype(BF)
    weights = w_ref[...]
    lane = iota((column, experts), 1)
    scale = jnp.zeros((column, experts), F32)
    for e in range(experts):
        named = jnp.sum(jnp.where(ids == first + e, weights, 0.0), axis=1, keepdims=True)
        scale = scale + jnp.where(lane == e, named, 0.0)
    scale_hi = scale.astype(BF)
    scale_lo = (scale - scale_hi.astype(F32)).astype(BF)
    expert, _, _ = row_fields(iota((experts, lanes), 1), chips_y)
    spread = (expert == iota((experts, lanes), 0)).astype(BF)
    far = dot(rank, spread).astype(BF)
    far_hi = dot(scale_hi, spread).astype(BF)
    far_lo = dot(scale_lo, spread).astype(BF)
    expert, part, slot = row_fields(iota((rows, lanes), 1), chips_y)
    same_part = part == iota((rows, lanes), 0) % SPLIT
    slot = slot.astype(F32)
    names = first + expert
    tok = iota((rows, column), 1)
    group = iota((rows, column), 0) // SPLIT
    top = ids.shape[1]
    route = iota((rows, top), 1) == iota((rows, top), 0) % SPLIT
    low = ids.astype(F32).astype(BF)
    for t in range(toks):
        at = (tok == group * toks + t).astype(BF)
        held = dot(at, far) == slot
        both = held & same_part
        hi_ref[t] = jnp.where(both, dot(at, far_hi), 0.0).astype(BF)
        lo_ref[t] = jnp.where(both, dot(at, far_lo), 0.0).astype(BF)
        name = jnp.sum(jnp.where(route, dot(at, low), 0.0), axis=1, keepdims=True)
        mine = name == names.astype(F32)
        pick_ref[t] = (held & mine & (part == 0)).astype(BF)


def pack_kernel(pick_ref, tokens_ref, o_ref):
    toks = pick_ref.shape[0]
    width = tokens_ref.shape[1] // toks
    total = dot(pick_ref[0], tokens_ref[:, :width])
    for t in range(1, toks):
        total = total + dot(pick_ref[t], tokens_ref[:, t * width : (t + 1) * width])
    o_ref[...] = total.astype(BF)


def scaled(value):
    largest = jnp.max(jnp.abs(value), axis=1, keepdims=True)
    power = jnp.where(largest > 0.0, jnp.floor(jnp.log2(jnp.maximum(largest, 1e-30))), 0.0)
    return value * jnp.exp2(-power), power


def partial_kernel(core_ref, rows_ref, go_ref, gt_ref, uo_ref, ut_ref, do_ref, dt_ref, o_ref):
    core = core_ref[0]
    both, width2 = rows_ref.shape
    width, hidden = go_ref.shape
    rows = both // 2
    q = iota((both, both), 0)
    half = jnp.where(q < rows, core, 1 - core)
    q = q % rows
    source = (q // MOST) * ROWS + half * MOST + q % MOST
    order = (source == iota((both, both), 1)).astype(BF)
    held = dot(order, rows_ref[...]).astype(BF)
    x_own, x_other = held[:rows, :width], held[rows:, :width]
    g_own, g_other = held[:rows, width:], held[rows:, width:]
    gate, gate_power = scaled(dot(x_own, go_ref[...]) + dot(x_other, gt_ref[...]))
    o_ref[:, :hidden] = gate
    up, up_power = scaled(dot(x_own, uo_ref[...]) + dot(x_other, ut_ref[...]))
    o_ref[:, hidden : 2 * hidden] = up
    down, down_power = scaled(dot_t(g_own, do_ref[...]) + dot_t(g_other, dt_ref[...]))
    o_ref[:, 2 * hidden : 3 * hidden] = down
    lane = iota((rows, 128), 1)
    powers = jnp.where(lane == 0, gate_power, jnp.where(lane == 1, up_power, down_power))
    o_ref[:, 3 * hidden :] = powers


def hidden_kernel(hidden, p_ref, o_ref):
    def total(which):
        value = None
        for j in range(p_ref.shape[0]):
            at = 3 * hidden + which
            factor = jnp.exp2(p_ref[j, :, 3 * hidden :][:, which : which + 1])
            term = p_ref[j, :, which * hidden : (which + 1) * hidden] * factor
            value = term if value is None else value + term
        return value

    a, b, r = total(0), total(1), total(2)
    sig = jax.nn.sigmoid(a)
    silu = a * sig
    o_ref[:, :hidden] = (r * b * (sig * (1.0 + a * (1.0 - sig)))).astype(BF)
    o_ref[:, hidden : 2 * hidden] = (r * silu).astype(BF)
    route = jnp.sum(silu * b * r, axis=1, keepdims=True)
    hi = route.astype(BF).astype(F32)
    mid = (route - hi).astype(BF).astype(F32)
    lo = route - hi - mid
    lane = iota((route.shape[0], 128), 1)
    pieces = jnp.where(lane == 0, hi, jnp.where(lane == 1, mid, jnp.where(lane == 2, lo, 0.0)))
    o_ref[:, 2 * hidden :] = pieces.astype(BF)


def return_kernel(core_ref, d_ref, go_ref, gt_ref, uo_ref, ut_ref, o_ref):
    core = core_ref[0]
    width, hidden = go_ref.shape
    rows = d_ref.shape[0]
    d_gate = d_ref[:, :hidden]
    d_up = d_ref[:, hidden : 2 * hidden]
    own = (dot_t(d_gate, go_ref[...]) + dot_t(d_up, uo_ref[...])).astype(BF)
    other = (dot_t(d_gate, gt_ref[...]) + dot_t(d_up, ut_ref[...])).astype(BF)
    q = iota((2 * rows, rows), 0)
    here = (q // ROWS) * MOST + q % MOST == iota((2 * rows, rows), 1)
    mine = (q // MOST) % 2 == core
    to_own = (here & mine).astype(BF)
    to_other = (here & ~mine).astype(BF)
    o_ref[:, :width] = (dot(to_own, own) + dot(to_other, other)).astype(BF)
    o_ref[:, width:] = dot(here.astype(BF), d_ref[:, 2 * hidden :]).astype(BF)


def combine_kernel(hi_ref, lo_ref, pick_ref, b_ref, o_ref):
    toks, rows, _ = hi_ref.shape
    width = b_ref.shape[1] - 128
    value = b_ref[:, :width]
    extra = b_ref[:, width:]
    lane = iota((rows, 128), 1)
    routes = jnp.zeros((rows, 128), F32)
    for t in range(toks):
        total = dot(hi_ref[t], value) + dot(lo_ref[t], value)
        o_ref[:, t * width : (t + 1) * width] = total.astype(BF)
        route = jnp.sum(dot(pick_ref[t], extra), axis=1, keepdims=True)
        hi = route.astype(BF).astype(F32)
        routes = jnp.where(lane == 2 * t, hi, jnp.where(lane == 2 * t + 1, route - hi, routes))
    o_ref[:, toks * width :] = routes.astype(BF)


def home_kernel(toks, width, h_ref, x_ref, r_ref):
    total = h_ref[0].astype(F32)
    for g in range(1, h_ref.shape[0]):
        total = total + h_ref[g].astype(F32)
    top = r_ref.shape[1]
    extra = total[:, toks * width :]
    lane = iota(extra.shape, 1)
    diagonal = iota((SPLIT, top), 0) == iota((SPLIT, top), 1)
    for t in range(toks):
        for s in range(SPLIT):
            x_ref[t : t + 1, s * width : (s + 1) * width] = total[
                s : s + 1, t * width : (t + 1) * width
            ]
        route = jnp.sum(jnp.where(lane // 2 == t, extra, 0.0), axis=1, keepdims=True)
        r_ref[t : t + 1, :] = jnp.sum(jnp.where(diagonal, route, 0.0), axis=0, keepdims=True)


def body(grad_out, inputs, expert_ids, route_weights, w_gate, w_up, w_down):
    groups = lax.axis_size("z")
    chips_y = lax.axis_size("yl")
    experts = lax.axis_size("x") * lax.axis_size("yh")
    chips = experts * chips_y
    toks = grad_out.shape[1]
    width, hidden = w_gate.shape[1:]
    top = expert_ids.shape[2]
    core = lax.axis_index("c").astype(jnp.int32).reshape(1)
    first = (lax.axis_index("z") * experts).astype(jnp.int32).reshape(1)
    held = groups * SPLIT
    sent = chips * ROWS
    rows = chips * MOST

    swap = [(0, 1), (1, 0)]
    wg, wu, wd = w_gate[0], w_up[0], w_down[0]
    wg_other = lax.ppermute(wg, "c", swap)
    wu_other = lax.ppermute(wu, "c", swap)
    wd_other = lax.ppermute(wd, "c", swap)

    payload = call(
        functools.partial(payload_kernel, toks, width),
        jax.ShapeDtypeStruct((SPLIT, 2 * toks * width), BF),
        16,
        inputs[0],
        grad_out[0],
    )
    tokens = lax.all_gather(payload, "z", axis=0, tiled=False).reshape(held, -1)

    pick = call(
        functools.partial(pick_kernel, toks, experts, chips_y),
        jax.ShapeDtypeStruct((toks, sent, held), BF),
        16,
        first,
        expert_ids[0],
        smem=1,
    )
    merged = jax.ShapeDtypeStruct((toks, held, sent), BF)
    merge_hi, merge_lo, merge_pick = call(
        functools.partial(merge_kernel, toks, experts, chips_y),
        [merged, merged, merged],
        16,
        first,
        expert_ids[0],
        route_weights[0],
        smem=1,
    )

    packed = call(pack_kernel, jax.ShapeDtypeStruct((sent, 2 * width), BF), 16, pick, tokens)
    got = lax.all_to_all(
        packed.reshape(chips, ROWS, 2 * width), CHIPS, split_axis=0, concat_axis=0, tiled=True
    ).reshape(sent, 2 * width)

    partials = call(
        partial_kernel,
        jax.ShapeDtypeStruct((rows, 3 * hidden + 128), F32),
        32,
        core,
        got,
        wg,
        wg_other,
        wu,
        wu_other,
        wd,
        wd_other,
        smem=1,
    )
    shares = partials.astype(jnp.float16).reshape(chips_y, rows // chips_y, -1)
    shares = lax.all_to_all(shares, "yl", split_axis=0, concat_axis=0, tiled=True)
    grads = call(
        functools.partial(hidden_kernel, hidden),
        jax.ShapeDtypeStruct((rows // chips_y, 2 * hidden + 128), BF),
        16,
        shares.astype(F32),
    )
    all_grads = lax.all_gather(grads, "yl", axis=0, tiled=True)

    back = call(
        return_kernel,
        jax.ShapeDtypeStruct((sent, width + 128), BF),
        32,
        core,
        all_grads,
        wg,
        wg_other,
        wu,
        wu_other,
        smem=1,
    )
    back = lax.all_to_all(
        back.reshape(chips, ROWS, -1), CHIPS, split_axis=0, concat_axis=0, tiled=True
    ).reshape(sent, -1)

    home = call(
        combine_kernel,
        jax.ShapeDtypeStruct((held, toks * width + 128), BF),
        16,
        merge_hi,
        merge_lo,
        merge_pick,
        back,
    )
    home = lax.all_to_all(
        home.reshape(groups, SPLIT, -1), "z", split_axis=0, concat_axis=0, tiled=True
    )
    grad_in, grad_route = call(
        functools.partial(home_kernel, toks, width),
        [
            jax.ShapeDtypeStruct((toks, SPLIT * width), F32),
            jax.ShapeDtypeStruct((toks, top), F32),
        ],
        16,
        home,
    )
    return grad_in[None], grad_route[None]


def solution(mesh):
    groups, members = mesh.devices.shape
    chips_y = SPLIT // 2
    x = 4 if members == 64 else 2
    fine = Mesh(
        mesh.devices.reshape(groups, x, members // (x * SPLIT), chips_y, 2), ("z",) + CORES
    )
    tokens = P(CORES, "z", None)
    tables = P(CORES, None, None)
    weights = P(("z",) + CORES, None, None)
    return jax.shard_map(
        body,
        mesh=fine,
        in_specs=(tokens, tokens, tables, tables, weights, weights, weights),
        out_specs=(tokens, tokens),
        check_vma=False,
    )
```

```python
import functools

import jax
import jax.numpy as jnp
from jax import lax
from jax.experimental import pallas as pl
from jax.experimental.pallas import tpu as pltpu
from jax.sharding import Mesh, PartitionSpec as P

BF = jnp.bfloat16
F32 = jnp.float32
MOST = 4
SPLIT = 8
ROWS = 2 * MOST
CORES = ("x", "yh", "yl", "c")
CHIPS = ("x", "yh", "yl")
ABT = (((1,), (1,)), ((), ()))


def dot(a, b):
    return jnp.dot(a, b, preferred_element_type=F32)


def dot_t(a, b):
    return lax.dot_general(a, b, ABT, preferred_element_type=F32)


def iota(shape, axis):
    return lax.broadcasted_iota(jnp.int32, shape, axis)


def call(kernel, out, limit_mib, *args, smem=0, hbm=0, scratch=()):
    inside = len(args) - smem - hbm
    spaces = [pltpu.SMEM] * smem + [pltpu.VMEM] * inside + [pltpu.HBM] * hbm
    many = isinstance(out, (list, tuple))
    outs = [pl.BlockSpec(memory_space=pltpu.VMEM) for _ in out] if many else None
    return pl.pallas_call(
        kernel,
        out_shape=out,
        in_specs=[pl.BlockSpec(memory_space=space) for space in spaces],
        out_specs=outs if many else pl.BlockSpec(memory_space=pltpu.VMEM),
        scratch_shapes=scratch,
        compiler_params=pltpu.CompilerParams(vmem_limit_bytes=limit_mib << 20),
    )(*args)


def weight_places(width, hidden):
    return (
        (pl.ds(0, width), pl.ds(width, hidden)),
        (pl.ds(width, width), pl.ds(width, hidden)),
        (pl.ds(0, hidden), pl.ds(0, width)),
    )


def bring(source, room, sems, places):
    copies = [
        pltpu.make_async_copy(source.at[place], room.at[place], sems.at[i])
        for i, place in enumerate(places)
    ]
    for copy in copies:
        copy.start()
    return copies


def start_kernel(toks, x_hbm, g_hbm, wg_hbm, wu_hbm, wd_hbm, o_ref, all_hbm, held, room, sems):
    width, hidden = wg_hbm.shape[1:]
    copies = [
        pltpu.make_async_copy(ref, held.at[i], sems.at[i]) for i, ref in enumerate((x_hbm, g_hbm))
    ]
    moves = [
        (
            pltpu.make_async_copy(ref.at[0], room.at[place], sems.at[2 + i]),
            pltpu.make_async_copy(room.at[place], all_hbm.at[place], sems.at[5 + i]),
        )
        for i, (ref, place) in enumerate(
            zip((wg_hbm, wu_hbm, wd_hbm), weight_places(width, hidden))
        )
    ]
    for copy in copies + [come for come, _ in moves]:
        copy.start()
    for tensor, copy in enumerate(copies):
        copy.wait()
        value = held[tensor, 0].astype(F32)
        for t in range(toks):
            rows = [value[t : t + 1, s * width : (s + 1) * width] for s in range(SPLIT)]
            at = (t * 2 + tensor) * width
            o_ref[:, at : at + width] = jnp.concatenate(rows, axis=0).astype(BF)
    for come, go in moves:
        come.wait()
        go.start()
    for _, go in moves:
        go.wait()


def spread_rows(rows):
    at = iota((len(rows), rows[0].shape[1]), 0)
    value = jnp.zeros(at.shape, F32)
    for e, row in enumerate(rows):
        value = value + jnp.where(at == e, row, 0.0)
    return value


def rank_table(ids, first, experts):
    column = ids.shape[1]
    match = spread_rows(
        [
            jnp.sum((ids == first + e).astype(F32), axis=0, keepdims=True)
            for e in range(experts)
        ]
    )
    earlier = (iota((column, column), 0) < iota((column, column), 1)).astype(BF)
    rank = dot(match.astype(BF), earlier)
    return jnp.where(match > 0.0, rank, -1.0)


def row_fields(index, chips_y):
    slot = index % MOST
    part = (index // MOST) % (2 * chips_y)
    return index // (MOST * 2 * chips_y), part, slot


def pick_kernel(toks, experts, chips_y, first_ref, ids_ref, o_ref):
    _, rows, lanes = o_ref.shape
    column = ids_ref.shape[1]
    rank = rank_table(ids_ref[...], first_ref[0], experts).astype(BF)
    expert, _, _ = row_fields(iota((rows, experts), 0), chips_y)
    spread = dot((expert == iota((rows, experts), 1)).astype(BF), rank).astype(BF)
    _, part, slot = row_fields(iota((rows, lanes), 0), chips_y)
    same_part = part == iota((rows, lanes), 1) % SPLIT
    tok = iota((column, lanes), 0)
    group = iota((column, lanes), 1) // SPLIT
    for t in range(toks):
        table = dot(spread, (tok == group * toks + t).astype(BF))
        o_ref[t] = (same_part & (table == slot.astype(F32))).astype(BF)


def merge_kernel(toks, experts, chips_y, first_ref, ids_ref, w_ref, hi_ref, lo_ref, pick_ref):
    _, rows, lanes = hi_ref.shape
    column = ids_ref.shape[1]
    ids = ids_ref[...]
    first = first_ref[0]
    rank = rank_table(ids, first, experts).astype(BF)
    weights = w_ref[...]
    scale = spread_rows(
        [
            jnp.sum(jnp.where(ids == first + e, weights, 0.0), axis=0, keepdims=True)
            for e in range(experts)
        ]
    )
    scale_hi = scale.astype(BF)
    scale_lo = (scale - scale_hi.astype(F32)).astype(BF)
    expert, _, _ = row_fields(iota((experts, lanes), 1), chips_y)
    spread = (expert == iota((experts, lanes), 0)).astype(BF)
    expert, part, slot = row_fields(iota((rows, lanes), 1), chips_y)
    same_part = part == iota((rows, lanes), 0) % SPLIT
    slot = slot.astype(F32)
    names = (first + expert).astype(F32)
    tok = iota((rows, column), 1)
    group = iota((rows, column), 0) // SPLIT
    top = ids.shape[0]
    route = iota((rows, top), 1) == iota((rows, top), 0) % SPLIT
    low = ids.astype(F32).astype(BF)
    for t in range(toks):
        at = (tok == group * toks + t).astype(BF)
        held = dot(dot_t(at, rank).astype(BF), spread) == slot
        both = held & same_part
        hi_ref[t] = jnp.where(both, dot(dot_t(at, scale_hi).astype(BF), spread), 0.0).astype(BF)
        lo_ref[t] = jnp.where(both, dot(dot_t(at, scale_lo).astype(BF), spread), 0.0).astype(BF)
        name = jnp.sum(jnp.where(route, dot_t(at, low), 0.0), axis=1, keepdims=True)
        pick_ref[t] = (held & (name == names) & (part == 0)).astype(BF)


def pack_kernel(pick_ref, tokens_ref, o_ref):
    toks = pick_ref.shape[0]
    groups, split, lanes = tokens_ref.shape
    width = lanes // toks
    total = None
    for t in range(toks):
        tokens = tokens_ref[:, :, t * width : (t + 1) * width].reshape(groups * split, width)
        term = dot(pick_ref[t], tokens)
        total = term if total is None else total + term
    o_ref[...] = total.astype(BF)


def scaled(value):
    largest = jnp.max(jnp.abs(value), axis=1, keepdims=True)
    power = jnp.where(largest > 0.0, jnp.floor(jnp.log2(jnp.maximum(largest, 1e-30))), 0.0)
    return value * jnp.exp2(-power), power


def partial_kernel(core_ref, rows_ref, own_ref, other_hbm, o_ref, other_ref, sems):
    core = core_ref[0]
    both = rows_ref.shape[0]
    hidden = own_ref.shape[0]
    width = own_ref.shape[1] - hidden
    places = weight_places(width, hidden)
    copies = bring(other_hbm, other_ref, sems, places)
    rows = both // 2
    q = iota((both, both), 0)
    half = jnp.where(q < rows, core, 1 - core)
    q = q % rows
    source = (q // MOST) * ROWS + half * MOST + q % MOST
    order = (source == iota((both, both), 1)).astype(BF)
    held = dot(order, rows_ref[...]).astype(BF)
    x_own, x_other = held[:rows, :width], held[rows:, :width]
    g_own, g_other = held[:rows, width:], held[rows:, width:]
    gate = dot(x_own, own_ref[:width, width:])
    up = dot(x_own, own_ref[width:, width:])
    down = dot_t(g_own, own_ref[:, :width])
    copies[0].wait()
    gate, gate_power = scaled(gate + dot(x_other, other_ref[:width, width:]))
    o_ref[:, :hidden] = gate
    copies[1].wait()
    up, up_power = scaled(up + dot(x_other, other_ref[width:, width:]))
    o_ref[:, hidden : 2 * hidden] = up
    copies[2].wait()
    down, down_power = scaled(down + dot_t(g_other, other_ref[:, :width]))
    o_ref[:, 2 * hidden : 3 * hidden] = down
    lane = iota((rows, 128), 1)
    powers = jnp.where(lane == 0, gate_power, jnp.where(lane == 1, up_power, down_power))
    o_ref[:, 3 * hidden :] = powers


def hidden_kernel(hidden, p_ref, o_ref):
    def total(which):
        value = None
        for j in range(p_ref.shape[0]):
            at = 3 * hidden + which
            factor = jnp.exp2(p_ref[j, :, 3 * hidden :][:, which : which + 1])
            term = p_ref[j, :, which * hidden : (which + 1) * hidden] * factor
            value = term if value is None else value + term
        return value

    a, b, r = total(0), total(1), total(2)
    sig = jax.nn.sigmoid(a)
    silu = a * sig
    o_ref[:, :hidden] = (r * b * (sig * (1.0 + a * (1.0 - sig)))).astype(BF)
    o_ref[:, hidden : 2 * hidden] = (r * silu).astype(BF)
    route = jnp.sum(silu * b * r, axis=1, keepdims=True)
    hi = route.astype(BF).astype(F32)
    mid = (route - hi).astype(BF).astype(F32)
    lo = route - hi - mid
    lane = iota((route.shape[0], 128), 1)
    pieces = jnp.where(lane == 0, hi, jnp.where(lane == 1, mid, jnp.where(lane == 2, lo, 0.0)))
    o_ref[:, 2 * hidden :] = pieces.astype(BF)


def return_kernel(core_ref, d_ref, own_ref, other_hbm, o_ref, other_ref, sems):
    core = core_ref[0]
    hidden = own_ref.shape[0]
    width = own_ref.shape[1] - hidden
    copies = bring(other_hbm, other_ref, sems, weight_places(width, hidden)[:2])
    rows = d_ref.shape[0] * d_ref.shape[1]
    grads = d_ref[...].reshape(rows, -1)
    d_gate = grads[:, :hidden]
    d_up = grads[:, hidden : 2 * hidden]
    own = (dot_t(d_gate, own_ref[:width, width:]) + dot_t(d_up, own_ref[width:, width:])).astype(BF)
    for copy in copies:
        copy.wait()
    other = (
        dot_t(d_gate, other_ref[:width, width:]) + dot_t(d_up, other_ref[width:, width:])
    ).astype(BF)
    q = iota((2 * rows, rows), 0)
    here = (q // ROWS) * MOST + q % MOST == iota((2 * rows, rows), 1)
    mine = (q // MOST) % 2 == core
    to_own = (here & mine).astype(BF)
    to_other = (here & ~mine).astype(BF)
    o_ref[:, :width] = (dot(to_own, own) + dot(to_other, other)).astype(BF)
    o_ref[:, width:] = dot(here.astype(BF), grads[:, 2 * hidden :]).astype(BF)


def combine_kernel(hi_ref, lo_ref, pick_ref, b_ref, o_ref):
    toks, rows, _ = hi_ref.shape
    width = b_ref.shape[1] - 128
    value = b_ref[:, :width]
    extra = b_ref[:, width:]
    lane = iota((rows, 128), 1)
    routes = jnp.zeros((rows, 128), F32)
    for t in range(toks):
        total = dot(hi_ref[t], value) + dot(lo_ref[t], value)
        o_ref[:, t * width : (t + 1) * width] = total.astype(BF)
        route = jnp.sum(dot(pick_ref[t], extra), axis=1, keepdims=True)
        hi = route.astype(BF).astype(F32)
        routes = jnp.where(lane == 2 * t, hi, jnp.where(lane == 2 * t + 1, route - hi, routes))
    o_ref[:, toks * width :] = routes.astype(BF)


def home_kernel(toks, width, h_ref, x_ref, r_ref):
    total = h_ref[0].astype(F32)
    for g in range(1, h_ref.shape[0]):
        total = total + h_ref[g].astype(F32)
    top = r_ref.shape[2]
    extra = total[:, toks * width :]
    lane = iota(extra.shape, 1)
    diagonal = iota((SPLIT, top), 0) == iota((SPLIT, top), 1)
    for t in range(toks):
        for s in range(SPLIT):
            x_ref[t, :, s * width : (s + 1) * width] = total[
                s : s + 1, t * width : (t + 1) * width
            ]
        route = jnp.sum(jnp.where(lane // 2 == t, extra, 0.0), axis=1, keepdims=True)
        r_ref[t] = jnp.sum(jnp.where(diagonal, route, 0.0), axis=0, keepdims=True)


def body(grad_out, inputs, expert_ids, route_weights, w_gate, w_up, w_down):
    groups = lax.axis_size("z")
    chips_y = lax.axis_size("yl")
    experts = lax.axis_size("x") * lax.axis_size("yh")
    chips = experts * chips_y
    toks = grad_out.shape[1]
    width, hidden = w_gate.shape[1:]
    top = expert_ids.shape[2]
    core = lax.axis_index("c").astype(jnp.int32).reshape(1)
    first = (lax.axis_index("z") * experts).astype(jnp.int32).reshape(1)
    held = groups * SPLIT
    sent = chips * ROWS
    rows = chips * MOST

    swap = [(0, 1), (1, 0)]

    payload, weights = pl.pallas_call(
        functools.partial(start_kernel, toks),
        out_shape=[
            jax.ShapeDtypeStruct((SPLIT, 2 * toks * width), BF),
            jax.ShapeDtypeStruct((hidden, width + hidden), BF),
        ],
        in_specs=[pl.BlockSpec(memory_space=pltpu.HBM)] * 5,
        out_specs=[
            pl.BlockSpec(memory_space=pltpu.VMEM),
            pl.BlockSpec(memory_space=pltpu.HBM),
        ],
        scratch_shapes=[
            pltpu.VMEM((2,) + inputs.shape, BF),
            pltpu.VMEM((hidden, width + hidden), BF),
            pltpu.SemaphoreType.DMA((8,)),
        ],
        compiler_params=pltpu.CompilerParams(vmem_limit_bytes=60 << 20),
    )(inputs, grad_out, w_gate, w_up, w_down)
    other = lax.ppermute(weights, "c", swap)
    tokens = lax.all_gather(payload, "z", axis=0, tiled=False)

    pick = call(
        functools.partial(pick_kernel, toks, experts, chips_y),
        jax.ShapeDtypeStruct((toks, sent, held), BF),
        8,
        first,
        expert_ids[0].T,
        smem=1,
    )
    merged = jax.ShapeDtypeStruct((toks, held, sent), BF)
    merge_hi, merge_lo, merge_pick = call(
        functools.partial(merge_kernel, toks, experts, chips_y),
        [merged, merged, merged],
        8,
        first,
        expert_ids[0].T,
        route_weights[0].T,
        smem=1,
    )

    packed = call(pack_kernel, jax.ShapeDtypeStruct((sent, 2 * width), BF), 8, pick, tokens)
    got = lax.all_to_all(
        packed.reshape(chips, ROWS, 2 * width), CHIPS, split_axis=0, concat_axis=0, tiled=True
    ).reshape(sent, 2 * width)

    partials = call(
        partial_kernel,
        jax.ShapeDtypeStruct((rows, 3 * hidden + 128), F32),
        20,
        core,
        got,
        weights,
        other,
        smem=1,
        hbm=1,
        scratch=[pltpu.VMEM(weights.shape, BF), pltpu.SemaphoreType.DMA((3,))],
    )
    shares = partials.astype(jnp.float16).reshape(chips_y, rows // chips_y, -1)
    shares = lax.all_to_all(shares, "yl", split_axis=0, concat_axis=0, tiled=True)
    grads = call(
        functools.partial(hidden_kernel, hidden),
        jax.ShapeDtypeStruct((rows // chips_y, 2 * hidden + 128), BF),
        8,
        shares.astype(F32),
    )
    all_grads = lax.all_gather(grads, "yl", axis=0, tiled=False)

    back = call(
        return_kernel,
        jax.ShapeDtypeStruct((sent, width + 128), BF),
        20,
        core,
        all_grads,
        weights,
        other,
        smem=1,
        hbm=1,
        scratch=[pltpu.VMEM(weights.shape, BF), pltpu.SemaphoreType.DMA((3,))],
    )
    back = lax.all_to_all(
        back.reshape(chips, ROWS, -1), CHIPS, split_axis=0, concat_axis=0, tiled=True
    ).reshape(sent, -1)

    home = call(
        combine_kernel,
        jax.ShapeDtypeStruct((held, toks * width + 128), BF),
        8,
        merge_hi,
        merge_lo,
        merge_pick,
        back,
    )
    home = lax.all_to_all(
        home.reshape(groups, SPLIT, -1), "z", split_axis=0, concat_axis=0, tiled=True
    )
    grad_in, grad_route = call(
        functools.partial(home_kernel, toks, width),
        [
            jax.ShapeDtypeStruct((toks, 1, SPLIT * width), F32),
            jax.ShapeDtypeStruct((toks, 1, top), F32),
        ],
        8,
        home,
    )
    return jnp.swapaxes(grad_in, 0, 1), jnp.swapaxes(grad_route, 0, 1)


def solution(mesh):
    groups, members = mesh.devices.shape
    chips_y = SPLIT // 2
    x = 4 if members == 64 else 2
    fine = Mesh(
        mesh.devices.reshape(groups, x, members // (x * SPLIT), chips_y, 2), ("z",) + CORES
    )
    tokens = P(CORES, "z", None)
    tables = P(CORES, None, None)
    weights = P(("z",) + CORES, None, None)
    return jax.shard_map(
        body,
        mesh=fine,
        in_specs=(tokens, tokens, tables, tables, weights, weights, weights),
        out_specs=(tokens, tokens),
        check_vma=False,
    )
```

```python
import functools

import jax
import jax.numpy as jnp
from jax import lax
from jax.experimental import pallas as pl
from jax.experimental.pallas import tpu as pltpu
from jax.sharding import Mesh, PartitionSpec as P

BF = jnp.bfloat16
F32 = jnp.float32
MOST = 4
SPLIT = 8
ROWS = 2 * MOST
CORES = ("x", "yh", "yl", "c")
CHIPS = ("x", "yh", "yl")
ABT = (((1,), (1,)), ((), ()))


def dot(a, b):
    return jnp.dot(a, b, preferred_element_type=F32)


def dot_t(a, b):
    return lax.dot_general(a, b, ABT, preferred_element_type=F32)


def iota(shape, axis):
    return lax.broadcasted_iota(jnp.int32, shape, axis)


def call(kernel, out, limit_mib, *args, smem=0):
    spaces = [pltpu.SMEM] * smem + [pltpu.VMEM] * (len(args) - smem)
    many = isinstance(out, (list, tuple))
    outs = [pl.BlockSpec(memory_space=pltpu.VMEM) for _ in out] if many else None
    return pl.pallas_call(
        kernel,
        out_shape=out,
        in_specs=[pl.BlockSpec(memory_space=space) for space in spaces],
        out_specs=outs if many else pl.BlockSpec(memory_space=pltpu.VMEM),
        compiler_params=pltpu.CompilerParams(vmem_limit_bytes=limit_mib << 20),
    )(*args)


def payload_kernel(toks, width, x_hbm, g_hbm, o_ref, held, sems):
    copies = [
        pltpu.make_async_copy(ref, held.at[i], sems.at[i]) for i, ref in enumerate((x_hbm, g_hbm))
    ]
    for copy in copies:
        copy.start()
    for tensor, copy in enumerate(copies):
        copy.wait()
        value = held[tensor, 0].astype(F32)
        for t in range(toks):
            rows = [value[t : t + 1, s * width : (s + 1) * width] for s in range(SPLIT)]
            at = (t * 2 + tensor) * width
            o_ref[:, at : at + width] = jnp.concatenate(rows, axis=0).astype(BF)


def spread_rows(rows):
    at = iota((len(rows), rows[0].shape[1]), 0)
    value = jnp.zeros(at.shape, F32)
    for e, row in enumerate(rows):
        value = value + jnp.where(at == e, row, 0.0)
    return value


def rank_table(ids, first, experts):
    column = ids.shape[1]
    match = spread_rows(
        [
            jnp.sum((ids == first + e).astype(F32), axis=0, keepdims=True)
            for e in range(experts)
        ]
    )
    earlier = (iota((column, column), 0) < iota((column, column), 1)).astype(BF)
    rank = dot(match.astype(BF), earlier)
    return jnp.where(match > 0.0, rank, -1.0)


def row_fields(index, chips_y):
    slot = index % MOST
    part = (index // MOST) % (2 * chips_y)
    return index // (MOST * 2 * chips_y), part, slot


def pick_kernel(toks, experts, chips_y, place_ref, ids_ref, o_ref):
    _, rows, lanes = o_ref.shape
    column = ids_ref.shape[1]
    rank = rank_table(ids_ref[...], place_ref[0], experts).astype(BF)
    expert, _, _ = row_fields(iota((rows, experts), 0), chips_y)
    spread = dot((expert == iota((rows, experts), 1)).astype(BF), rank).astype(BF)
    _, part, slot = row_fields(iota((rows, lanes), 0), chips_y)
    same_part = part == iota((rows, lanes), 1) % SPLIT
    tok = iota((column, lanes), 0)
    group = iota((column, lanes), 1) // SPLIT
    for t in range(toks):
        table = dot(spread, (tok == group * toks + t).astype(BF))
        o_ref[t] = (same_part & (table == slot.astype(F32))).astype(BF)


def merge_kernel(toks, experts, chips_y, place_ref, ids_ref, w_ref, hi_ref, lo_ref, pick_ref):
    _, rows, lanes = hi_ref.shape
    column = ids_ref.shape[1]
    ids = ids_ref[...]
    first = place_ref[0]
    rank = rank_table(ids, first, experts).astype(BF)
    weights = w_ref[...]
    scale = spread_rows(
        [
            jnp.sum(jnp.where(ids == first + e, weights, 0.0), axis=0, keepdims=True)
            for e in range(experts)
        ]
    )
    scale_hi = scale.astype(BF)
    scale_lo = (scale - scale_hi.astype(F32)).astype(BF)
    expert, _, _ = row_fields(iota((experts, lanes), 1), chips_y)
    spread = (expert == iota((experts, lanes), 0)).astype(BF)
    expert, part, slot = row_fields(iota((rows, lanes), 1), chips_y)
    same_part = part == iota((rows, lanes), 0) % SPLIT
    slot = slot.astype(F32)
    names = (first + expert).astype(F32)
    tok = iota((rows, column), 1)
    group = iota((rows, column), 0) // SPLIT
    top = ids.shape[0]
    route = iota((rows, top), 1) == iota((rows, top), 0) % SPLIT
    low = ids.astype(F32).astype(BF)
    for t in range(toks):
        at = (tok == group * toks + t).astype(BF)
        held = dot(dot_t(at, rank).astype(BF), spread) == slot
        both = held & same_part
        hi_ref[t] = jnp.where(both, dot(dot_t(at, scale_hi).astype(BF), spread), 0.0).astype(BF)
        lo_ref[t] = jnp.where(both, dot(dot_t(at, scale_lo).astype(BF), spread), 0.0).astype(BF)
        name = jnp.sum(jnp.where(route, dot_t(at, low), 0.0), axis=1, keepdims=True)
        pick_ref[t] = (held & (name == names) & (part == 0)).astype(BF)


def pack_kernel(pick_ref, tokens_ref, o_ref):
    toks = pick_ref.shape[0]
    groups, split, lanes = tokens_ref.shape
    width = lanes // toks
    total = None
    for t in range(toks):
        tokens = tokens_ref[:, :, t * width : (t + 1) * width].reshape(groups * split, width)
        term = dot(pick_ref[t], tokens)
        total = term if total is None else total + term
    o_ref[...] = total.astype(BF)


def scaled(value):
    largest = jnp.max(jnp.abs(value), axis=1, keepdims=True)
    power = jnp.where(largest > 0.0, jnp.floor(jnp.log2(jnp.maximum(largest, 1e-30))), 0.0)
    return value * jnp.exp2(-power), power


def partial_kernel(place_ref, rows_ref, own_ref, other_ref, o_ref):
    core = place_ref[1]
    both = rows_ref.shape[0]
    hidden = own_ref.shape[0]
    width = own_ref.shape[1] - hidden
    rows = both // 2
    q = iota((both, both), 0)
    half = jnp.where(q < rows, core, 1 - core)
    q = q % rows
    source = (q // MOST) * ROWS + half * MOST + q % MOST
    order = (source == iota((both, both), 1)).astype(BF)
    held = dot(order, rows_ref[...]).astype(BF)
    x_own, x_other = held[:rows, :width], held[rows:, :width]
    g_own, g_other = held[:rows, width:], held[rows:, width:]
    gate = dot(x_own, own_ref[:width, width:])
    up = dot(x_own, own_ref[width:, width:])
    down = dot_t(g_own, own_ref[:, :width])
    gate, gate_power = scaled(gate + dot(x_other, other_ref[:width, width:]))
    o_ref[:, :hidden] = gate
    up, up_power = scaled(up + dot(x_other, other_ref[width:, width:]))
    o_ref[:, hidden : 2 * hidden] = up
    down, down_power = scaled(down + dot_t(g_other, other_ref[:, :width]))
    o_ref[:, 2 * hidden : 3 * hidden] = down
    lane = iota((rows, 128), 1)
    powers = jnp.where(lane == 0, gate_power, jnp.where(lane == 1, up_power, down_power))
    o_ref[:, 3 * hidden :] = powers


def hidden_kernel(hidden, p_ref, o_ref):
    def total(which):
        value = None
        for j in range(p_ref.shape[0]):
            at = 3 * hidden + which
            factor = jnp.exp2(p_ref[j, :, 3 * hidden :][:, which : which + 1])
            term = p_ref[j, :, which * hidden : (which + 1) * hidden] * factor
            value = term if value is None else value + term
        return value

    a, b, r = total(0), total(1), total(2)
    sig = jax.nn.sigmoid(a)
    silu = a * sig
    o_ref[:, :hidden] = (r * b * (sig * (1.0 + a * (1.0 - sig)))).astype(BF)
    o_ref[:, hidden : 2 * hidden] = (r * silu).astype(BF)
    route = jnp.sum(silu * b * r, axis=1, keepdims=True)
    hi = route.astype(BF).astype(F32)
    mid = (route - hi).astype(BF).astype(F32)
    lo = route - hi - mid
    lane = iota((route.shape[0], 128), 1)
    pieces = jnp.where(lane == 0, hi, jnp.where(lane == 1, mid, jnp.where(lane == 2, lo, 0.0)))
    o_ref[:, 2 * hidden :] = pieces.astype(BF)


def return_kernel(place_ref, d_ref, own_ref, other_ref, o_ref):
    core = place_ref[1]
    hidden = own_ref.shape[0]
    width = own_ref.shape[1] - hidden
    rows = d_ref.shape[0] * d_ref.shape[1]
    grads = d_ref[...].reshape(rows, -1)
    d_gate = grads[:, :hidden]
    d_up = grads[:, hidden : 2 * hidden]
    own = (dot_t(d_gate, own_ref[:width, width:]) + dot_t(d_up, own_ref[width:, width:])).astype(BF)
    other = (
        dot_t(d_gate, other_ref[:width, width:]) + dot_t(d_up, other_ref[width:, width:])
    ).astype(BF)
    q = iota((2 * rows, rows), 0)
    here = (q // ROWS) * MOST + q % MOST == iota((2 * rows, rows), 1)
    mine = (q // MOST) % 2 == core
    to_own = (here & mine).astype(BF)
    to_other = (here & ~mine).astype(BF)
    o_ref[:, :width] = (dot(to_own, own) + dot(to_other, other)).astype(BF)
    o_ref[:, width:] = dot(here.astype(BF), grads[:, 2 * hidden :]).astype(BF)


def combine_kernel(hi_ref, lo_ref, pick_ref, b_ref, o_ref):
    toks, rows, _ = hi_ref.shape
    width = b_ref.shape[1] - 128
    value = b_ref[:, :width]
    extra = b_ref[:, width:]
    lane = iota((rows, 128), 1)
    routes = jnp.zeros((rows, 128), F32)
    for t in range(toks):
        total = dot(hi_ref[t], value) + dot(lo_ref[t], value)
        o_ref[:, t * width : (t + 1) * width] = total.astype(BF)
        route = jnp.sum(dot(pick_ref[t], extra), axis=1, keepdims=True)
        hi = route.astype(BF).astype(F32)
        routes = jnp.where(lane == 2 * t, hi, jnp.where(lane == 2 * t + 1, route - hi, routes))
    o_ref[:, toks * width :] = routes.astype(BF)


def home_kernel(toks, width, h_ref, x_ref, r_ref):
    total = h_ref[0].astype(F32)
    for g in range(1, h_ref.shape[0]):
        total = total + h_ref[g].astype(F32)
    top = r_ref.shape[2]
    extra = total[:, toks * width :]
    lane = iota(extra.shape, 1)
    diagonal = iota((SPLIT, top), 0) == iota((SPLIT, top), 1)
    for t in range(toks):
        for s in range(SPLIT):
            x_ref[t, :, s * width : (s + 1) * width] = total[
                s : s + 1, t * width : (t + 1) * width
            ]
        route = jnp.sum(jnp.where(lane // 2 == t, extra, 0.0), axis=1, keepdims=True)
        r_ref[t] = jnp.sum(jnp.where(diagonal, route, 0.0), axis=0, keepdims=True)


def body(grad_out, inputs, expert_ids, route_weights, w_gate, w_up, w_down):
    groups = lax.axis_size("z")
    chips_y = lax.axis_size("yl")
    experts = lax.axis_size("x") * lax.axis_size("yh")
    chips = experts * chips_y
    toks = grad_out.shape[1]
    width, hidden = w_gate.shape[1:]
    top = expert_ids.shape[2]
    place = jnp.stack([lax.axis_index("z") * experts, lax.axis_index("c")]).astype(jnp.int32)
    held = groups * SPLIT
    sent = chips * ROWS
    rows = chips * MOST

    swap = [(0, 1), (1, 0)]

    place, down = lax.optimization_barrier((place, w_down[0]))
    weights = jnp.concatenate([down, jnp.concatenate([w_gate[0], w_up[0]], axis=0)], axis=1)
    payload = pl.pallas_call(
        functools.partial(payload_kernel, toks, width),
        out_shape=jax.ShapeDtypeStruct((SPLIT, 2 * toks * width), BF),
        in_specs=[pl.BlockSpec(memory_space=pltpu.HBM)] * 2,
        out_specs=pl.BlockSpec(memory_space=pltpu.VMEM),
        scratch_shapes=[
            pltpu.VMEM((2,) + inputs.shape, BF),
            pltpu.SemaphoreType.DMA((2,)),
        ],
        compiler_params=pltpu.CompilerParams(vmem_limit_bytes=4 << 20),
    )(inputs, grad_out)
    other = lax.ppermute(weights, "c", swap)
    tokens = lax.all_gather(payload, "z", axis=0, tiled=False)

    pick = call(
        functools.partial(pick_kernel, toks, experts, chips_y),
        jax.ShapeDtypeStruct((toks, sent, held), BF),
        8,
        place,
        expert_ids[0].T,
        smem=1,
    )
    merged = jax.ShapeDtypeStruct((toks, held, sent), BF)
    merge_hi, merge_lo, merge_pick = call(
        functools.partial(merge_kernel, toks, experts, chips_y),
        [merged, merged, merged],
        8,
        place,
        expert_ids[0].T,
        route_weights[0].T,
        smem=1,
    )

    packed = call(pack_kernel, jax.ShapeDtypeStruct((sent, 2 * width), BF), 8, pick, tokens)
    got = lax.all_to_all(
        packed.reshape(chips, ROWS, 2 * width), CHIPS, split_axis=0, concat_axis=0, tiled=True
    ).reshape(sent, 2 * width)

    partials = call(
        partial_kernel,
        jax.ShapeDtypeStruct((rows, 3 * hidden + 128), F32),
        20,
        place,
        got,
        weights,
        other,
        smem=1,
    )
    shares = partials.astype(jnp.float16).reshape(chips_y, rows // chips_y, -1)
    shares = lax.all_to_all(shares, "yl", split_axis=0, concat_axis=0, tiled=True)
    grads = call(
        functools.partial(hidden_kernel, hidden),
        jax.ShapeDtypeStruct((rows // chips_y, 2 * hidden + 128), BF),
        8,
        shares.astype(F32),
    )
    all_grads = lax.all_gather(grads, "yl", axis=0, tiled=False)

    back = call(
        return_kernel,
        jax.ShapeDtypeStruct((sent, width + 128), BF),
        20,
        place,
        all_grads,
        weights,
        other,
        smem=1,
    )
    back = lax.all_to_all(
        back.reshape(chips, ROWS, -1), CHIPS, split_axis=0, concat_axis=0, tiled=True
    ).reshape(sent, -1)

    home = call(
        combine_kernel,
        jax.ShapeDtypeStruct((held, toks * width + 128), BF),
        8,
        merge_hi,
        merge_lo,
        merge_pick,
        back,
    )
    home = lax.all_to_all(
        home.reshape(groups, SPLIT, -1), "z", split_axis=0, concat_axis=0, tiled=True
    )
    grad_in, grad_route = call(
        functools.partial(home_kernel, toks, width),
        [
            jax.ShapeDtypeStruct((toks, 1, SPLIT * width), F32),
            jax.ShapeDtypeStruct((toks, 1, top), F32),
        ],
        8,
        home,
    )
    return jnp.swapaxes(grad_in, 0, 1), jnp.swapaxes(grad_route, 0, 1)


def solution(mesh):
    groups, members = mesh.devices.shape
    chips_y = SPLIT // 2
    x = 4 if members == 64 else 2
    fine = Mesh(
        mesh.devices.reshape(groups, x, members // (x * SPLIT), chips_y, 2), ("z",) + CORES
    )
    tokens = P(CORES, "z", None)
    tables = P(CORES, None, None)
    weights = P(("z",) + CORES, None, None)
    return jax.shard_map(
        body,
        mesh=fine,
        in_specs=(tokens, tokens, tables, tables, weights, weights, weights),
        out_specs=(tokens, tokens),
        check_vma=False,
    )
```

```python
import functools

import jax
import jax.numpy as jnp
from jax import lax
from jax.experimental import pallas as pl
from jax.experimental.pallas import tpu as pltpu
from jax.sharding import Mesh, PartitionSpec as P

BF = jnp.bfloat16
F32 = jnp.float32
MOST = 4
SPLIT = 8
ROWS = 2 * MOST
CORES = ("x", "yh", "yl", "c")
CHIPS = ("x", "yh", "yl")
ABT = (((1,), (1,)), ((), ()))


def dot(a, b):
    return jnp.dot(a, b, preferred_element_type=F32)


def dot_t(a, b):
    return lax.dot_general(a, b, ABT, preferred_element_type=F32)


def iota(shape, axis):
    return lax.broadcasted_iota(jnp.int32, shape, axis)


def call(kernel, out, limit_mib, *args):
    many = isinstance(out, (list, tuple))
    outs = [pl.BlockSpec(memory_space=pltpu.VMEM) for _ in out] if many else None
    return pl.pallas_call(
        kernel,
        out_shape=out,
        in_specs=[pl.BlockSpec(memory_space=pltpu.VMEM) for _ in args],
        out_specs=outs if many else pl.BlockSpec(memory_space=pltpu.VMEM),
        compiler_params=pltpu.CompilerParams(vmem_limit_bytes=limit_mib << 20),
    )(*args)


def payload_kernel(toks, width, x_hbm, g_hbm, o_ref, held, sems):
    copies = [
        pltpu.make_async_copy(ref, held.at[i], sems.at[i]) for i, ref in enumerate((x_hbm, g_hbm))
    ]
    for copy in copies:
        copy.start()
    for tensor, copy in enumerate(copies):
        copy.wait()
        value = held[tensor, 0].astype(F32)
        for t in range(toks):
            rows = [value[t : t + 1, s * width : (s + 1) * width] for s in range(SPLIT)]
            at = (t * 2 + tensor) * width
            o_ref[:, at : at + width] = jnp.concatenate(rows, axis=0).astype(BF)


def spread_rows(rows):
    at = iota((len(rows), rows[0].shape[1]), 0)
    value = jnp.zeros(at.shape, F32)
    for e, row in enumerate(rows):
        value = value + jnp.where(at == e, row, 0.0)
    return value


def rank_table(ids, first, experts):
    column = ids.shape[1]
    match = spread_rows(
        [
            jnp.sum((ids == first + e).astype(F32), axis=0, keepdims=True)
            for e in range(experts)
        ]
    )
    earlier = (iota((column, column), 0) < iota((column, column), 1)).astype(BF)
    rank = dot(match.astype(BF), earlier)
    return jnp.where(match > 0.0, rank, -1.0)


def row_fields(index, chips_y):
    slot = index % MOST
    part = (index // MOST) % (2 * chips_y)
    return index // (MOST * 2 * chips_y), part, slot


def pick_kernel(toks, experts, chips_y, ids_ref, o_ref):
    _, rows, lanes = o_ref.shape
    column = ids_ref.shape[1]
    rank = rank_table(ids_ref[...], lax.axis_index("z") * experts, experts).astype(BF)
    expert, _, _ = row_fields(iota((rows, experts), 0), chips_y)
    spread = dot((expert == iota((rows, experts), 1)).astype(BF), rank).astype(BF)
    _, part, slot = row_fields(iota((rows, lanes), 0), chips_y)
    same_part = part == iota((rows, lanes), 1) % SPLIT
    tok = iota((column, lanes), 0)
    group = iota((column, lanes), 1) // SPLIT
    for t in range(toks):
        table = dot(spread, (tok == group * toks + t).astype(BF))
        o_ref[t] = (same_part & (table == slot.astype(F32))).astype(BF)


def merge_kernel(toks, experts, chips_y, ids_ref, w_ref, hi_ref, lo_ref, pick_ref):
    _, rows, lanes = hi_ref.shape
    column = ids_ref.shape[1]
    ids = ids_ref[...]
    first = lax.axis_index("z") * experts
    rank = rank_table(ids, first, experts).astype(BF)
    weights = w_ref[...]
    scale = spread_rows(
        [
            jnp.sum(jnp.where(ids == first + e, weights, 0.0), axis=0, keepdims=True)
            for e in range(experts)
        ]
    )
    scale_hi = scale.astype(BF)
    scale_lo = (scale - scale_hi.astype(F32)).astype(BF)
    expert, _, _ = row_fields(iota((experts, lanes), 1), chips_y)
    spread = (expert == iota((experts, lanes), 0)).astype(BF)
    expert, part, slot = row_fields(iota((rows, lanes), 1), chips_y)
    same_part = part == iota((rows, lanes), 0) % SPLIT
    slot = slot.astype(F32)
    names = (first + expert).astype(F32)
    tok = iota((rows, column), 1)
    group = iota((rows, column), 0) // SPLIT
    top = ids.shape[0]
    route = iota((rows, top), 1) == iota((rows, top), 0) % SPLIT
    low = ids.astype(F32).astype(BF)
    for t in range(toks):
        at = (tok == group * toks + t).astype(BF)
        held = dot(dot_t(at, rank).astype(BF), spread) == slot
        both = held & same_part
        hi_ref[t] = jnp.where(both, dot(dot_t(at, scale_hi).astype(BF), spread), 0.0).astype(BF)
        lo_ref[t] = jnp.where(both, dot(dot_t(at, scale_lo).astype(BF), spread), 0.0).astype(BF)
        name = jnp.sum(jnp.where(route, dot_t(at, low), 0.0), axis=1, keepdims=True)
        pick_ref[t] = (held & (name == names) & (part == 0)).astype(BF)


def pack_kernel(pick_ref, tokens_ref, o_ref):
    toks = pick_ref.shape[0]
    groups, split, lanes = tokens_ref.shape
    width = lanes // toks
    total = None
    for t in range(toks):
        tokens = tokens_ref[:, :, t * width : (t + 1) * width].reshape(groups * split, width)
        term = dot(pick_ref[t], tokens)
        total = term if total is None else total + term
    o_ref[...] = total.astype(BF)


def scaled(value):
    largest = jnp.max(jnp.abs(value), axis=1, keepdims=True)
    power = jnp.where(largest > 0.0, jnp.floor(jnp.log2(jnp.maximum(largest, 1e-30))), 0.0)
    return value * jnp.exp2(-power), power


def partial_kernel(rows_ref, own_ref, other_ref, o_ref):
    core = lax.axis_index("c")
    both = rows_ref.shape[0]
    hidden = own_ref.shape[0]
    width = own_ref.shape[1] - hidden
    rows = both // 2
    q = iota((both, both), 0)
    half = jnp.where(q < rows, core, 1 - core)
    q = q % rows
    source = (q // MOST) * ROWS + half * MOST + q % MOST
    order = (source == iota((both, both), 1)).astype(BF)
    held = dot(order, rows_ref[...]).astype(BF)
    x_own, x_other = held[:rows, :width], held[rows:, :width]
    g_own, g_other = held[:rows, width:], held[rows:, width:]
    gate = dot(x_own, own_ref[:width, width:])
    up = dot(x_own, own_ref[width:, width:])
    down = dot_t(g_own, own_ref[:, :width])
    gate, gate_power = scaled(gate + dot(x_other, other_ref[:width, width:]))
    o_ref[:, :hidden] = gate
    up, up_power = scaled(up + dot(x_other, other_ref[width:, width:]))
    o_ref[:, hidden : 2 * hidden] = up
    down, down_power = scaled(down + dot_t(g_other, other_ref[:, :width]))
    o_ref[:, 2 * hidden : 3 * hidden] = down
    lane = iota((rows, 128), 1)
    powers = jnp.where(lane == 0, gate_power, jnp.where(lane == 1, up_power, down_power))
    o_ref[:, 3 * hidden :] = powers


def hidden_kernel(hidden, p_ref, o_ref):
    def total(which):
        value = None
        for j in range(p_ref.shape[0]):
            at = 3 * hidden + which
            factor = jnp.exp2(p_ref[j, :, 3 * hidden :][:, which : which + 1])
            term = p_ref[j, :, which * hidden : (which + 1) * hidden] * factor
            value = term if value is None else value + term
        return value

    a, b, r = total(0), total(1), total(2)
    sig = jax.nn.sigmoid(a)
    silu = a * sig
    o_ref[:, :hidden] = (r * b * (sig * (1.0 + a * (1.0 - sig)))).astype(BF)
    o_ref[:, hidden : 2 * hidden] = (r * silu).astype(BF)
    route = jnp.sum(silu * b * r, axis=1, keepdims=True)
    hi = route.astype(BF).astype(F32)
    mid = (route - hi).astype(BF).astype(F32)
    lo = route - hi - mid
    lane = iota((route.shape[0], 128), 1)
    pieces = jnp.where(lane == 0, hi, jnp.where(lane == 1, mid, jnp.where(lane == 2, lo, 0.0)))
    o_ref[:, 2 * hidden :] = pieces.astype(BF)


def return_kernel(d_ref, own_ref, other_ref, o_ref):
    core = lax.axis_index("c")
    hidden = own_ref.shape[0]
    width = own_ref.shape[1] - hidden
    rows = d_ref.shape[0] * d_ref.shape[1]
    grads = d_ref[...].reshape(rows, -1)
    d_gate = grads[:, :hidden]
    d_up = grads[:, hidden : 2 * hidden]
    own = (dot_t(d_gate, own_ref[:width, width:]) + dot_t(d_up, own_ref[width:, width:])).astype(BF)
    other = (
        dot_t(d_gate, other_ref[:width, width:]) + dot_t(d_up, other_ref[width:, width:])
    ).astype(BF)
    q = iota((2 * rows, rows), 0)
    here = (q // ROWS) * MOST + q % MOST == iota((2 * rows, rows), 1)
    mine = (q // MOST) % 2 == core
    to_own = (here & mine).astype(BF)
    to_other = (here & ~mine).astype(BF)
    o_ref[:, :width] = (dot(to_own, own) + dot(to_other, other)).astype(BF)
    o_ref[:, width:] = dot(here.astype(BF), grads[:, 2 * hidden :]).astype(BF)


def combine_kernel(hi_ref, lo_ref, pick_ref, b_ref, o_ref):
    toks, rows, _ = hi_ref.shape
    width = b_ref.shape[1] - 128
    value = b_ref[:, :width]
    extra = b_ref[:, width:]
    lane = iota((rows, 128), 1)
    routes = jnp.zeros((rows, 128), F32)
    for t in range(toks):
        total = dot(hi_ref[t], value) + dot(lo_ref[t], value)
        o_ref[:, t * width : (t + 1) * width] = total.astype(BF)
        route = jnp.sum(dot(pick_ref[t], extra), axis=1, keepdims=True)
        hi = route.astype(BF).astype(F32)
        routes = jnp.where(lane == 2 * t, hi, jnp.where(lane == 2 * t + 1, route - hi, routes))
    o_ref[:, toks * width :] = routes.astype(BF)


def home_kernel(toks, width, h_ref, x_ref, r_ref):
    total = h_ref[0].astype(F32)
    for g in range(1, h_ref.shape[0]):
        total = total + h_ref[g].astype(F32)
    top = r_ref.shape[2]
    extra = total[:, toks * width :]
    lane = iota(extra.shape, 1)
    diagonal = iota((SPLIT, top), 0) == iota((SPLIT, top), 1)
    for t in range(toks):
        for s in range(SPLIT):
            x_ref[t, :, s * width : (s + 1) * width] = total[
                s : s + 1, t * width : (t + 1) * width
            ]
        route = jnp.sum(jnp.where(lane // 2 == t, extra, 0.0), axis=1, keepdims=True)
        r_ref[t] = jnp.sum(jnp.where(diagonal, route, 0.0), axis=0, keepdims=True)


def body(grad_out, inputs, expert_ids, route_weights, w_gate, w_up, w_down):
    groups = lax.axis_size("z")
    chips_y = lax.axis_size("yl")
    experts = lax.axis_size("x") * lax.axis_size("yh")
    chips = experts * chips_y
    toks = grad_out.shape[1]
    width, hidden = w_gate.shape[1:]
    top = expert_ids.shape[2]
    held = groups * SPLIT
    sent = chips * ROWS
    rows = chips * MOST

    swap = [(0, 1), (1, 0)]

    weights = jnp.concatenate([w_down[0], jnp.concatenate([w_gate[0], w_up[0]], axis=0)], axis=1)
    payload = pl.pallas_call(
        functools.partial(payload_kernel, toks, width),
        out_shape=jax.ShapeDtypeStruct((SPLIT, 2 * toks * width), BF),
        in_specs=[pl.BlockSpec(memory_space=pltpu.HBM)] * 2,
        out_specs=pl.BlockSpec(memory_space=pltpu.VMEM),
        scratch_shapes=[
            pltpu.VMEM((2,) + inputs.shape, BF),
            pltpu.SemaphoreType.DMA((2,)),
        ],
        compiler_params=pltpu.CompilerParams(vmem_limit_bytes=4 << 20),
    )(inputs, grad_out)
    other = lax.ppermute(weights, "c", swap)
    tokens = lax.all_gather(payload, "z", axis=0, tiled=False)

    pick = call(
        functools.partial(pick_kernel, toks, experts, chips_y),
        jax.ShapeDtypeStruct((toks, sent, held), BF),
        8,
        expert_ids[0].T,
    )
    merged = jax.ShapeDtypeStruct((toks, held, sent), BF)
    merge_hi, merge_lo, merge_pick = call(
        functools.partial(merge_kernel, toks, experts, chips_y),
        [merged, merged, merged],
        8,
        expert_ids[0].T,
        route_weights[0].T,
    )

    packed = call(pack_kernel, jax.ShapeDtypeStruct((sent, 2 * width), BF), 8, pick, tokens)
    got = lax.all_to_all(
        packed.reshape(chips, ROWS, 2 * width), CHIPS, split_axis=0, concat_axis=0, tiled=True
    ).reshape(sent, 2 * width)

    partials = call(
        partial_kernel,
        jax.ShapeDtypeStruct((rows, 3 * hidden + 128), F32),
        20,
        got,
        weights,
        other,
    )
    shares = partials.astype(jnp.float16).reshape(chips_y, rows // chips_y, -1)
    shares = lax.all_to_all(shares, "yl", split_axis=0, concat_axis=0, tiled=True)
    grads = call(
        functools.partial(hidden_kernel, hidden),
        jax.ShapeDtypeStruct((rows // chips_y, 2 * hidden + 128), BF),
        8,
        shares.astype(F32),
    )
    all_grads = lax.all_gather(grads, "yl", axis=0, tiled=False)

    back = call(
        return_kernel,
        jax.ShapeDtypeStruct((sent, width + 128), BF),
        20,
        all_grads,
        weights,
        other,
    )
    back = lax.all_to_all(
        back.reshape(chips, ROWS, -1), CHIPS, split_axis=0, concat_axis=0, tiled=True
    ).reshape(sent, -1)

    home = call(
        combine_kernel,
        jax.ShapeDtypeStruct((held, toks * width + 128), BF),
        8,
        merge_hi,
        merge_lo,
        merge_pick,
        back,
    )
    home = lax.all_to_all(
        home.reshape(groups, SPLIT, -1), "z", split_axis=0, concat_axis=0, tiled=True
    )
    grad_in, grad_route = call(
        functools.partial(home_kernel, toks, width),
        [
            jax.ShapeDtypeStruct((toks, 1, SPLIT * width), F32),
            jax.ShapeDtypeStruct((toks, 1, top), F32),
        ],
        8,
        home,
    )
    return jnp.swapaxes(grad_in, 0, 1), jnp.swapaxes(grad_route, 0, 1)


def solution(mesh):
    groups, members = mesh.devices.shape
    chips_y = SPLIT // 2
    x = 4 if members == 64 else 2
    fine = Mesh(
        mesh.devices.reshape(groups, x, members // (x * SPLIT), chips_y, 2), ("z",) + CORES
    )
    tokens = P(CORES, "z", None)
    tables = P(CORES, None, None)
    weights = P(("z",) + CORES, None, None)
    return jax.shard_map(
        body,
        mesh=fine,
        in_specs=(tokens, tokens, tables, tables, weights, weights, weights),
        out_specs=(tokens, tokens),
        check_vma=False,
    )
```

```python
import functools

import jax
import jax.numpy as jnp
from jax import lax
from jax.experimental import pallas as pl
from jax.experimental.pallas import tpu as pltpu
from jax.sharding import Mesh, PartitionSpec as P

BF = jnp.bfloat16
F32 = jnp.float32
MOST = 4
SPLIT = 8
ROWS = 2 * MOST
CORES = ("x", "yh", "yl", "c")
CHIPS = ("x", "yh", "yl")
ABT = (((1,), (1,)), ((), ()))


def dot(a, b):
    return jnp.dot(a, b, preferred_element_type=F32)


def dot_t(a, b):
    return lax.dot_general(a, b, ABT, preferred_element_type=F32)


def iota(shape, axis):
    return lax.broadcasted_iota(jnp.int32, shape, axis)


def call(kernel, out, limit_mib, *args):
    many = isinstance(out, (list, tuple))
    outs = [pl.BlockSpec(memory_space=pltpu.VMEM) for _ in out] if many else None
    return pl.pallas_call(
        kernel,
        out_shape=out,
        in_specs=[pl.BlockSpec(memory_space=pltpu.VMEM) for _ in args],
        out_specs=outs if many else pl.BlockSpec(memory_space=pltpu.VMEM),
        compiler_params=pltpu.CompilerParams(vmem_limit_bytes=limit_mib << 20),
    )(*args)


def payload_kernel(toks, width, x_hbm, g_hbm, o_ref, held, sems):
    copies = [
        pltpu.make_async_copy(ref, held.at[i], sems.at[i]) for i, ref in enumerate((x_hbm, g_hbm))
    ]
    for copy in copies:
        copy.start()
    for tensor, copy in enumerate(copies):
        copy.wait()
        value = held[tensor, 0].astype(F32)
        for t in range(toks):
            rows = [value[t : t + 1, s * width : (s + 1) * width] for s in range(SPLIT)]
            at = (t * 2 + tensor) * width
            o_ref[:, at : at + width] = jnp.concatenate(rows, axis=0).astype(BF)


def spread_rows(rows):
    at = iota((len(rows), rows[0].shape[1]), 0)
    value = jnp.zeros(at.shape, F32)
    for e, row in enumerate(rows):
        value = value + jnp.where(at == e, row, 0.0)
    return value


def rank_table(ids, first, experts):
    column = ids.shape[1]
    match = spread_rows(
        [
            jnp.sum((ids == first + e).astype(F32), axis=0, keepdims=True)
            for e in range(experts)
        ]
    )
    earlier = (iota((column, column), 0) < iota((column, column), 1)).astype(BF)
    rank = dot(match.astype(BF), earlier)
    return jnp.where(match > 0.0, rank, -1.0)


def row_fields(index, chips_y):
    slot = index % MOST
    part = (index // MOST) % (2 * chips_y)
    return index // (MOST * 2 * chips_y), part, slot


def pick_kernel(toks, experts, chips_y, ids_ref, o_ref):
    _, rows, lanes = o_ref.shape
    column = ids_ref.shape[1]
    rank = rank_table(ids_ref[...], lax.axis_index("z") * experts, experts).astype(BF)
    expert, _, _ = row_fields(iota((rows, experts), 0), chips_y)
    spread = dot((expert == iota((rows, experts), 1)).astype(BF), rank).astype(BF)
    _, part, slot = row_fields(iota((rows, lanes), 0), chips_y)
    same_part = part == iota((rows, lanes), 1) % SPLIT
    tok = iota((column, lanes), 0)
    group = iota((column, lanes), 1) // SPLIT
    for t in range(toks):
        table = dot(spread, (tok == group * toks + t).astype(BF))
        o_ref[t] = (same_part & (table == slot.astype(F32))).astype(BF)


def merge_kernel(toks, experts, chips_y, ids_ref, w_ref, hi_ref, lo_ref, pick_ref):
    _, rows, lanes = hi_ref.shape
    column = ids_ref.shape[1]
    ids = ids_ref[...]
    first = lax.axis_index("z") * experts
    rank = rank_table(ids, first, experts).astype(BF)
    weights = w_ref[...]
    scale = spread_rows(
        [
            jnp.sum(jnp.where(ids == first + e, weights, 0.0), axis=0, keepdims=True)
            for e in range(experts)
        ]
    )
    scale_hi = scale.astype(BF)
    scale_lo = (scale - scale_hi.astype(F32)).astype(BF)
    expert, _, _ = row_fields(iota((experts, lanes), 1), chips_y)
    spread = (expert == iota((experts, lanes), 0)).astype(BF)
    expert, part, slot = row_fields(iota((rows, lanes), 1), chips_y)
    same_part = part == iota((rows, lanes), 0) % SPLIT
    slot = slot.astype(F32)
    names = (first + expert).astype(F32)
    tok = iota((rows, column), 1)
    group = iota((rows, column), 0) // SPLIT
    top = ids.shape[0]
    route = iota((rows, top), 1) == iota((rows, top), 0) % SPLIT
    low = ids.astype(F32).astype(BF)
    for t in range(toks):
        at = (tok == group * toks + t).astype(BF)
        held = dot(dot_t(at, rank).astype(BF), spread) == slot
        both = held & same_part
        hi_ref[t] = jnp.where(both, dot(dot_t(at, scale_hi).astype(BF), spread), 0.0).astype(BF)
        lo_ref[t] = jnp.where(both, dot(dot_t(at, scale_lo).astype(BF), spread), 0.0).astype(BF)
        name = jnp.sum(jnp.where(route, dot_t(at, low), 0.0), axis=1, keepdims=True)
        pick_ref[t] = (held & (name == names) & (part == 0)).astype(BF)


def pack_kernel(pick_ref, tokens_ref, o_ref):
    toks = pick_ref.shape[0]
    groups, split, lanes = tokens_ref.shape
    width = lanes // toks
    total = None
    for t in range(toks):
        tokens = tokens_ref[:, :, t * width : (t + 1) * width].reshape(groups * split, width)
        term = dot(pick_ref[t], tokens)
        total = term if total is None else total + term
    o_ref[...] = total.astype(BF)


def scaled(value):
    largest = jnp.max(jnp.abs(value), axis=1, keepdims=True)
    power = jnp.where(largest > 0.0, jnp.floor(jnp.log2(jnp.maximum(largest, 1e-30))), 0.0)
    return value * jnp.exp2(-power), power


def partial_kernel(rows_ref, own_ref, other_ref, o_ref):
    core = lax.axis_index("c")
    both = rows_ref.shape[0]
    hidden = own_ref.shape[0]
    width = own_ref.shape[1] - hidden
    rows = both // 2
    q = iota((both, both), 0)
    half = jnp.where(q < rows, core, 1 - core)
    q = q % rows
    source = (q // MOST) * ROWS + half * MOST + q % MOST
    order = (source == iota((both, both), 1)).astype(BF)
    held = dot(order, rows_ref[...]).astype(BF)
    x_own, x_other = held[:rows, :width], held[rows:, :width]
    g_own, g_other = held[:rows, width:], held[rows:, width:]
    gate = dot(x_own, own_ref[:width, width:])
    up = dot(x_own, own_ref[width:, width:])
    down = dot_t(g_own, own_ref[:, :width])
    gate, gate_power = scaled(gate + dot(x_other, other_ref[:width, width:]))
    o_ref[:, :hidden] = gate
    up, up_power = scaled(up + dot(x_other, other_ref[width:, width:]))
    o_ref[:, hidden : 2 * hidden] = up
    down, down_power = scaled(down + dot_t(g_other, other_ref[:, :width]))
    o_ref[:, 2 * hidden : 3 * hidden] = down
    lane = iota((rows, 128), 1)
    powers = jnp.where(lane == 0, gate_power, jnp.where(lane == 1, up_power, down_power))
    o_ref[:, 3 * hidden :] = powers


def hidden_kernel(hidden, p_ref, o_ref):
    def total(which):
        value = None
        for j in range(p_ref.shape[0]):
            at = 3 * hidden + which
            factor = jnp.exp2(p_ref[j, :, 3 * hidden :][:, which : which + 1])
            term = p_ref[j, :, which * hidden : (which + 1) * hidden] * factor
            value = term if value is None else value + term
        return value

    a, b, r = total(0), total(1), total(2)
    sig = jax.nn.sigmoid(a)
    silu = a * sig
    d_gate = (r * b * (sig * (1.0 + a * (1.0 - sig)))).astype(BF)
    d_up = (r * silu).astype(BF)
    route = jnp.sum(silu * b * r, axis=1, keepdims=True)
    hi = route.astype(BF).astype(F32)
    mid = (route - hi).astype(BF).astype(F32)
    lo = route - hi - mid
    lane = iota((route.shape[0], 128), 1)
    pieces = jnp.where(lane == 0, hi, jnp.where(lane == 1, mid, jnp.where(lane == 2, lo, 0.0)))
    for j in range(o_ref.shape[0]):
        o_ref[j, :, :hidden] = d_gate
        o_ref[j, :, hidden : 2 * hidden] = d_up
        o_ref[j, :, 2 * hidden :] = pieces.astype(BF)


def return_kernel(d_ref, own_ref, other_ref, o_ref):
    core = lax.axis_index("c")
    hidden = own_ref.shape[0]
    width = own_ref.shape[1] - hidden
    rows = d_ref.shape[0] * d_ref.shape[1]
    grads = d_ref[...].reshape(rows, -1)
    d_gate = grads[:, :hidden]
    d_up = grads[:, hidden : 2 * hidden]
    own = (dot_t(d_gate, own_ref[:width, width:]) + dot_t(d_up, own_ref[width:, width:])).astype(BF)
    other = (
        dot_t(d_gate, other_ref[:width, width:]) + dot_t(d_up, other_ref[width:, width:])
    ).astype(BF)
    q = iota((2 * rows, rows), 0)
    here = (q // ROWS) * MOST + q % MOST == iota((2 * rows, rows), 1)
    mine = (q // MOST) % 2 == core
    to_own = (here & mine).astype(BF)
    to_other = (here & ~mine).astype(BF)
    o_ref[:, :width] = (dot(to_own, own) + dot(to_other, other)).astype(BF)
    o_ref[:, width:] = dot(here.astype(BF), grads[:, 2 * hidden :]).astype(BF)


def combine_kernel(hi_ref, lo_ref, pick_ref, b_ref, o_ref):
    toks, rows, _ = hi_ref.shape
    width = b_ref.shape[1] - 128
    value = b_ref[:, :width]
    extra = b_ref[:, width:]
    lane = iota((rows, 128), 1)
    routes = jnp.zeros((rows, 128), F32)
    for t in range(toks):
        total = dot(hi_ref[t], value) + dot(lo_ref[t], value)
        o_ref[:, t * width : (t + 1) * width] = total.astype(BF)
        route = jnp.sum(dot(pick_ref[t], extra), axis=1, keepdims=True)
        hi = route.astype(BF).astype(F32)
        routes = jnp.where(lane == 2 * t, hi, jnp.where(lane == 2 * t + 1, route - hi, routes))
    o_ref[:, toks * width :] = routes.astype(BF)


def home_kernel(toks, width, h_ref, x_ref, r_ref):
    total = h_ref[0].astype(F32)
    for g in range(1, h_ref.shape[0]):
        total = total + h_ref[g].astype(F32)
    top = r_ref.shape[2]
    extra = total[:, toks * width :]
    lane = iota(extra.shape, 1)
    diagonal = iota((SPLIT, top), 0) == iota((SPLIT, top), 1)
    for t in range(toks):
        for s in range(SPLIT):
            x_ref[t, :, s * width : (s + 1) * width] = total[
                s : s + 1, t * width : (t + 1) * width
            ]
        route = jnp.sum(jnp.where(lane // 2 == t, extra, 0.0), axis=1, keepdims=True)
        r_ref[t] = jnp.sum(jnp.where(diagonal, route, 0.0), axis=0, keepdims=True)


def body(grad_out, inputs, expert_ids, route_weights, w_gate, w_up, w_down):
    groups = lax.axis_size("z")
    chips_y = lax.axis_size("yl")
    experts = lax.axis_size("x") * lax.axis_size("yh")
    chips = experts * chips_y
    toks = grad_out.shape[1]
    width, hidden = w_gate.shape[1:]
    top = expert_ids.shape[2]
    held = groups * SPLIT
    sent = chips * ROWS
    rows = chips * MOST

    swap = [(0, 1), (1, 0)]

    weights = jnp.concatenate([w_down[0], jnp.concatenate([w_gate[0], w_up[0]], axis=0)], axis=1)
    payload = pl.pallas_call(
        functools.partial(payload_kernel, toks, width),
        out_shape=jax.ShapeDtypeStruct((SPLIT, 2 * toks * width), BF),
        in_specs=[pl.BlockSpec(memory_space=pltpu.HBM)] * 2,
        out_specs=pl.BlockSpec(memory_space=pltpu.VMEM),
        scratch_shapes=[
            pltpu.VMEM((2,) + inputs.shape, BF),
            pltpu.SemaphoreType.DMA((2,)),
        ],
        compiler_params=pltpu.CompilerParams(vmem_limit_bytes=4 << 20),
    )(inputs, grad_out)
    other = lax.ppermute(weights, "c", swap)
    tokens = lax.all_gather(payload, "z", axis=0, tiled=False)

    pick = call(
        functools.partial(pick_kernel, toks, experts, chips_y),
        jax.ShapeDtypeStruct((toks, sent, held), BF),
        8,
        expert_ids[0].T,
    )
    merged = jax.ShapeDtypeStruct((toks, held, sent), BF)
    merge_hi, merge_lo, merge_pick = call(
        functools.partial(merge_kernel, toks, experts, chips_y),
        [merged, merged, merged],
        8,
        expert_ids[0].T,
        route_weights[0].T,
    )

    packed = call(pack_kernel, jax.ShapeDtypeStruct((sent, 2 * width), BF), 8, pick, tokens)
    got = lax.all_to_all(
        packed.reshape(chips, ROWS, 2 * width), CHIPS, split_axis=0, concat_axis=0, tiled=True
    ).reshape(sent, 2 * width)

    partials = call(
        partial_kernel,
        jax.ShapeDtypeStruct((rows, 3 * hidden + 128), F32),
        20,
        got,
        weights,
        other,
    )
    shares = partials.astype(jnp.float16).reshape(chips_y, rows // chips_y, -1)
    shares = lax.all_to_all(shares, "yl", split_axis=0, concat_axis=0, tiled=True)
    grads = call(
        functools.partial(hidden_kernel, hidden),
        jax.ShapeDtypeStruct((chips_y, rows // chips_y, 2 * hidden + 128), BF),
        8,
        shares.astype(F32),
    )
    all_grads = lax.all_to_all(grads, "yl", split_axis=0, concat_axis=0, tiled=True)

    back = call(
        return_kernel,
        jax.ShapeDtypeStruct((sent, width + 128), BF),
        20,
        all_grads,
        weights,
        other,
    )
    back = lax.all_to_all(
        back.reshape(chips, ROWS, -1), CHIPS, split_axis=0, concat_axis=0, tiled=True
    ).reshape(sent, -1)

    home = call(
        combine_kernel,
        jax.ShapeDtypeStruct((held, toks * width + 128), BF),
        8,
        merge_hi,
        merge_lo,
        merge_pick,
        back,
    )
    home = lax.all_to_all(
        home.reshape(groups, SPLIT, -1), "z", split_axis=0, concat_axis=0, tiled=True
    )
    grad_in, grad_route = call(
        functools.partial(home_kernel, toks, width),
        [
            jax.ShapeDtypeStruct((toks, 1, SPLIT * width), F32),
            jax.ShapeDtypeStruct((toks, 1, top), F32),
        ],
        8,
        home,
    )
    return jnp.swapaxes(grad_in, 0, 1), jnp.swapaxes(grad_route, 0, 1)


def solution(mesh):
    groups, members = mesh.devices.shape
    chips_y = SPLIT // 2
    x = 4 if members == 64 else 2
    fine = Mesh(
        mesh.devices.reshape(groups, x, members // (x * SPLIT), chips_y, 2), ("z",) + CORES
    )
    tokens = P(CORES, "z", None)
    tables = P(CORES, None, None)
    weights = P(("z",) + CORES, None, None)
    return jax.shard_map(
        body,
        mesh=fine,
        in_specs=(tokens, tokens, tables, tables, weights, weights, weights),
        out_specs=(tokens, tokens),
        check_vma=False,
    )
```

```python
import functools

import jax
import jax.numpy as jnp
from jax import lax
from jax.experimental import pallas as pl
from jax.experimental.pallas import tpu as pltpu
from jax.sharding import Mesh, PartitionSpec as P

BF = jnp.bfloat16
F32 = jnp.float32
MOST = 4
SPLIT = 8
ROWS = 2 * MOST
CORES = ("x", "yh", "yl", "c")
CHIPS = ("x", "yh", "yl")
ABT = (((1,), (1,)), ((), ()))


def dot(a, b):
    return jnp.dot(a, b, preferred_element_type=F32)


def dot_t(a, b):
    return lax.dot_general(a, b, ABT, preferred_element_type=F32)


def iota(shape, axis):
    return lax.broadcasted_iota(jnp.int32, shape, axis)


def call(kernel, out, limit_mib, *args):
    many = isinstance(out, (list, tuple))
    outs = [pl.BlockSpec(memory_space=pltpu.VMEM) for _ in out] if many else None
    return pl.pallas_call(
        kernel,
        out_shape=out,
        in_specs=[pl.BlockSpec(memory_space=pltpu.VMEM) for _ in args],
        out_specs=outs if many else pl.BlockSpec(memory_space=pltpu.VMEM),
        compiler_params=pltpu.CompilerParams(vmem_limit_bytes=limit_mib << 20),
    )(*args)


def payload_kernel(toks, width, x_hbm, g_hbm, o_ref, held, sems):
    copies = [
        pltpu.make_async_copy(ref, held.at[i], sems.at[i]) for i, ref in enumerate((x_hbm, g_hbm))
    ]
    for copy in copies:
        copy.start()
    for tensor, copy in enumerate(copies):
        copy.wait()
        value = held[tensor, 0].astype(F32)
        for t in range(toks):
            rows = [value[t : t + 1, s * width : (s + 1) * width] for s in range(SPLIT)]
            at = (t * 2 + tensor) * width
            o_ref[:, at : at + width] = jnp.concatenate(rows, axis=0).astype(BF)


def spread_rows(rows):
    at = iota((len(rows), rows[0].shape[1]), 0)
    value = jnp.zeros(at.shape, F32)
    for e, row in enumerate(rows):
        value = value + jnp.where(at == e, row, 0.0)
    return value


def rank_table(ids, first, experts):
    column = ids.shape[1]
    match = spread_rows(
        [
            jnp.sum((ids == first + e).astype(F32), axis=0, keepdims=True)
            for e in range(experts)
        ]
    )
    earlier = (iota((column, column), 0) < iota((column, column), 1)).astype(BF)
    rank = dot(match.astype(BF), earlier)
    return jnp.where(match > 0.0, rank, -1.0)


def row_fields(index, chips_y):
    slot = index % MOST
    part = (index // MOST) % (2 * chips_y)
    return index // (MOST * 2 * chips_y), part, slot


def pick_kernel(toks, experts, chips_y, ids_ref, o_ref):
    _, rows, lanes = o_ref.shape
    column = ids_ref.shape[1]
    rank = rank_table(ids_ref[...], lax.axis_index("z") * experts, experts).astype(BF)
    expert, _, _ = row_fields(iota((rows, experts), 0), chips_y)
    spread = dot((expert == iota((rows, experts), 1)).astype(BF), rank).astype(BF)
    _, part, slot = row_fields(iota((rows, lanes), 0), chips_y)
    same_part = part == iota((rows, lanes), 1) % SPLIT
    tok = iota((column, lanes), 0)
    group = iota((column, lanes), 1) // SPLIT
    for t in range(toks):
        table = dot(spread, (tok == group * toks + t).astype(BF))
        o_ref[t] = (same_part & (table == slot.astype(F32))).astype(BF)


def merge_kernel(toks, experts, chips_y, ids_ref, w_ref, hi_ref, lo_ref, pick_ref):
    _, rows, lanes = hi_ref.shape
    column = ids_ref.shape[1]
    ids = ids_ref[...]
    first = lax.axis_index("z") * experts
    rank = rank_table(ids, first, experts).astype(BF)
    weights = w_ref[...]
    scale = spread_rows(
        [
            jnp.sum(jnp.where(ids == first + e, weights, 0.0), axis=0, keepdims=True)
            for e in range(experts)
        ]
    )
    scale_hi = scale.astype(BF)
    scale_lo = (scale - scale_hi.astype(F32)).astype(BF)
    expert, _, _ = row_fields(iota((experts, lanes), 1), chips_y)
    spread = (expert == iota((experts, lanes), 0)).astype(BF)
    expert, part, slot = row_fields(iota((rows, lanes), 1), chips_y)
    same_part = part == iota((rows, lanes), 0) % SPLIT
    slot = slot.astype(F32)
    names = (first + expert).astype(F32)
    tok = iota((rows, column), 1)
    group = iota((rows, column), 0) // SPLIT
    top = ids.shape[0]
    route = iota((rows, top), 1) == iota((rows, top), 0) % SPLIT
    low = ids.astype(F32).astype(BF)
    for t in range(toks):
        at = (tok == group * toks + t).astype(BF)
        held = dot(dot_t(at, rank).astype(BF), spread) == slot
        both = held & same_part
        hi_ref[t] = jnp.where(both, dot(dot_t(at, scale_hi).astype(BF), spread), 0.0).astype(BF)
        lo_ref[t] = jnp.where(both, dot(dot_t(at, scale_lo).astype(BF), spread), 0.0).astype(BF)
        name = jnp.sum(jnp.where(route, dot_t(at, low), 0.0), axis=1, keepdims=True)
        pick_ref[t] = (held & (name == names) & (part == 0)).astype(BF)


def pack_kernel(pick_ref, tokens_ref, o_ref):
    toks = pick_ref.shape[0]
    groups, split, lanes = tokens_ref.shape
    width = lanes // toks
    total = None
    for t in range(toks):
        tokens = tokens_ref[:, :, t * width : (t + 1) * width].reshape(groups * split, width)
        term = dot(pick_ref[t], tokens)
        total = term if total is None else total + term
    o_ref[...] = total.astype(BF)


def scaled(value):
    largest = jnp.max(jnp.abs(value), axis=1, keepdims=True)
    power = jnp.where(largest > 0.0, jnp.floor(jnp.log2(jnp.maximum(largest, 1e-30))), 0.0)
    return value * jnp.exp2(-power), power


def partial_kernel(rows_ref, own_ref, other_ref, o_ref):
    core = lax.axis_index("c")
    both = rows_ref.shape[0]
    hidden = own_ref.shape[0]
    width = own_ref.shape[1] - hidden
    rows = both // 2
    q = iota((both, both), 0)
    half = jnp.where(q < rows, core, 1 - core)
    q = q % rows
    source = (q // MOST) * ROWS + half * MOST + q % MOST
    order = (source == iota((both, both), 1)).astype(BF)
    held = dot(order, rows_ref[...]).astype(BF)
    x_own, x_other = held[:rows, :width], held[rows:, :width]
    g_own, g_other = held[:rows, width:], held[rows:, width:]
    gate = dot(x_own, own_ref[:width, width:])
    up = dot(x_own, own_ref[width:, width:])
    down = dot_t(g_own, own_ref[:, :width])
    gate, gate_power = scaled(gate + dot(x_other, other_ref[:width, width:]))
    o_ref[:, :hidden] = gate
    up, up_power = scaled(up + dot(x_other, other_ref[width:, width:]))
    o_ref[:, hidden : 2 * hidden] = up
    down, down_power = scaled(down + dot_t(g_other, other_ref[:, :width]))
    o_ref[:, 2 * hidden : 3 * hidden] = down
    lane = iota((rows, 128), 1)
    powers = jnp.where(lane == 0, gate_power, jnp.where(lane == 1, up_power, down_power))
    o_ref[:, 3 * hidden :] = powers


def hidden_kernel(hidden, p_ref, o_ref):
    def total(which):
        value = None
        for j in range(p_ref.shape[0]):
            at = 3 * hidden + which
            factor = jnp.exp2(p_ref[j, :, 3 * hidden :][:, which : which + 1])
            term = p_ref[j, :, which * hidden : (which + 1) * hidden] * factor
            value = term if value is None else value + term
        return value

    a, b, r = total(0), total(1), total(2)
    sig = jax.nn.sigmoid(a)
    silu = a * sig
    d_gate = (r * b * (sig * (1.0 + a * (1.0 - sig)))).astype(BF)
    d_up = (r * silu).astype(BF)
    route = jnp.sum(silu * b * r, axis=1, keepdims=True)
    hi = route.astype(BF).astype(F32)
    mid = (route - hi).astype(BF).astype(F32)
    lo = route - hi - mid
    lane = iota((route.shape[0], 128), 1)
    pieces = jnp.where(lane == 0, hi, jnp.where(lane == 1, mid, jnp.where(lane == 2, lo, 0.0)))
    for j in range(o_ref.shape[0]):
        o_ref[j, :, :hidden] = d_gate
        o_ref[j, :, hidden : 2 * hidden] = d_up
        o_ref[j, :, 2 * hidden :] = pieces.astype(BF)


def return_kernel(d_ref, own_ref, other_ref, o_ref):
    core = lax.axis_index("c")
    hidden = own_ref.shape[0]
    width = own_ref.shape[1] - hidden
    rows = d_ref.shape[0] * d_ref.shape[1]
    grads = d_ref[...].reshape(rows, -1)
    d_gate = grads[:, :hidden]
    d_up = grads[:, hidden : 2 * hidden]
    own = (dot_t(d_gate, own_ref[:width, width:]) + dot_t(d_up, own_ref[width:, width:])).astype(BF)
    other = (
        dot_t(d_gate, other_ref[:width, width:]) + dot_t(d_up, other_ref[width:, width:])
    ).astype(BF)
    q = iota((2 * rows, rows), 0)
    here = (q // ROWS) * MOST + q % MOST == iota((2 * rows, rows), 1)
    mine = (q // MOST) % 2 == core
    to_own = (here & mine).astype(BF)
    to_other = (here & ~mine).astype(BF)
    o_ref[:, :width] = (dot(to_own, own) + dot(to_other, other)).astype(BF)
    o_ref[:, width:] = dot(here.astype(BF), grads[:, 2 * hidden :]).astype(BF)


def combine_kernel(hi_ref, lo_ref, pick_ref, b_ref, o_ref):
    toks, rows, _ = hi_ref.shape
    width = b_ref.shape[1] - 128
    value = b_ref[:, :width]
    extra = b_ref[:, width:]
    lane = iota((rows, 128), 1)
    routes = jnp.zeros((rows, 128), F32)
    for t in range(toks):
        total = dot(hi_ref[t], value) + dot(lo_ref[t], value)
        o_ref[:, t * width : (t + 1) * width] = total.astype(BF)
        route = jnp.sum(dot(pick_ref[t], extra), axis=1, keepdims=True)
        hi = route.astype(BF).astype(F32)
        routes = jnp.where(lane == 2 * t, hi, jnp.where(lane == 2 * t + 1, route - hi, routes))
    o_ref[:, toks * width :] = routes.astype(BF)


def home_kernel(toks, width, h_ref, x_ref, r_ref):
    total = h_ref[0].astype(F32)
    for g in range(1, h_ref.shape[0]):
        total = total + h_ref[g].astype(F32)
    top = r_ref.shape[2]
    extra = total[:, toks * width :]
    lane = iota(extra.shape, 1)
    diagonal = iota((SPLIT, top), 0) == iota((SPLIT, top), 1)
    for t in range(toks):
        for s in range(SPLIT):
            x_ref[t, :, s * width : (s + 1) * width] = total[
                s : s + 1, t * width : (t + 1) * width
            ]
        route = jnp.sum(jnp.where(lane // 2 == t, extra, 0.0), axis=1, keepdims=True)
        r_ref[t] = jnp.sum(jnp.where(diagonal, route, 0.0), axis=0, keepdims=True)


def body(grad_out, inputs, expert_ids, route_weights, w_gate, w_up, w_down):
    groups = lax.axis_size("z")
    chips_y = lax.axis_size("yl")
    experts = lax.axis_size("x") * lax.axis_size("yh")
    chips = experts * chips_y
    toks = grad_out.shape[1]
    width, hidden = w_gate.shape[1:]
    top = expert_ids.shape[2]
    held = groups * SPLIT
    sent = chips * ROWS
    rows = chips * MOST

    swap = [(0, 1), (1, 0)]

    weights = jnp.concatenate([w_down[0], jnp.concatenate([w_gate[0], w_up[0]], axis=0)], axis=1)
    payload = pl.pallas_call(
        functools.partial(payload_kernel, toks, width),
        out_shape=jax.ShapeDtypeStruct((SPLIT, 2 * toks * width), BF),
        in_specs=[pl.BlockSpec(memory_space=pltpu.HBM)] * 2,
        out_specs=pl.BlockSpec(memory_space=pltpu.VMEM),
        scratch_shapes=[
            pltpu.VMEM((2,) + inputs.shape, BF),
            pltpu.SemaphoreType.DMA((2,)),
        ],
        compiler_params=pltpu.CompilerParams(vmem_limit_bytes=4 << 20),
    )(inputs, grad_out)
    other = lax.ppermute(weights, "c", swap)
    tokens = lax.all_gather(payload, "z", axis=0, tiled=False)

    pick = call(
        functools.partial(pick_kernel, toks, experts, chips_y),
        jax.ShapeDtypeStruct((toks, sent, held), BF),
        8,
        expert_ids[0].T,
    )
    merged = jax.ShapeDtypeStruct((toks, held, sent), BF)
    merge_hi, merge_lo, merge_pick = call(
        functools.partial(merge_kernel, toks, experts, chips_y),
        [merged, merged, merged],
        8,
        expert_ids[0].T,
        route_weights[0].T,
    )

    tokens, merge_hi = lax.optimization_barrier((tokens, merge_hi))
    packed = call(pack_kernel, jax.ShapeDtypeStruct((sent, 2 * width), BF), 8, pick, tokens)
    got = lax.all_to_all(
        packed.reshape(chips, ROWS, 2 * width), CHIPS, split_axis=0, concat_axis=0, tiled=True
    ).reshape(sent, 2 * width)

    partials = call(
        partial_kernel,
        jax.ShapeDtypeStruct((rows, 3 * hidden + 128), F32),
        20,
        got,
        weights,
        other,
    )
    shares = partials.astype(jnp.float16).reshape(chips_y, rows // chips_y, -1)
    shares = lax.all_to_all(shares, "yl", split_axis=0, concat_axis=0, tiled=True)
    grads = call(
        functools.partial(hidden_kernel, hidden),
        jax.ShapeDtypeStruct((chips_y, rows // chips_y, 2 * hidden + 128), BF),
        8,
        shares.astype(F32),
    )
    all_grads = lax.all_to_all(grads, "yl", split_axis=0, concat_axis=0, tiled=True)

    back = call(
        return_kernel,
        jax.ShapeDtypeStruct((sent, width + 128), BF),
        20,
        all_grads,
        weights,
        other,
    )
    back = lax.all_to_all(
        back.reshape(chips, ROWS, -1), CHIPS, split_axis=0, concat_axis=0, tiled=True
    ).reshape(sent, -1)

    home = call(
        combine_kernel,
        jax.ShapeDtypeStruct((held, toks * width + 128), BF),
        8,
        merge_hi,
        merge_lo,
        merge_pick,
        back,
    )
    home = lax.all_to_all(
        home.reshape(groups, SPLIT, -1), "z", split_axis=0, concat_axis=0, tiled=True
    )
    grad_in, grad_route = call(
        functools.partial(home_kernel, toks, width),
        [
            jax.ShapeDtypeStruct((toks, 1, SPLIT * width), F32),
            jax.ShapeDtypeStruct((toks, 1, top), F32),
        ],
        8,
        home,
    )
    return jnp.swapaxes(grad_in, 0, 1), jnp.swapaxes(grad_route, 0, 1)


def solution(mesh):
    groups, members = mesh.devices.shape
    chips_y = SPLIT // 2
    x = 4 if members == 64 else 2
    fine = Mesh(
        mesh.devices.reshape(groups, x, members // (x * SPLIT), chips_y, 2), ("z",) + CORES
    )
    tokens = P(CORES, "z", None)
    tables = P(CORES, None, None)
    weights = P(("z",) + CORES, None, None)
    return jax.shard_map(
        body,
        mesh=fine,
        in_specs=(tokens, tokens, tables, tables, weights, weights, weights),
        out_specs=(tokens, tokens),
        check_vma=False,
    )
```
